128 devices in a mesh: gx: 16 (over y, z), gy: 8 (over x, core).
Axes of the slice: x: 4, y: 4, z: 4, core: 2. Of those that a mesh axis runs over, the one named last changes fastest.
Arguments:
- old_fields: float32 [18, 1024, 1024], P(None, 'gx', 'gy'), may hold values from -6 to 6
- send_block: int32 [128, 256], P(('gx', 'gy')), may hold values from -1 to 63, as said below
- pair_slot: int32 [128, 112], P(('gx', 'gy')), may hold values from 0 to 255, as said below
- pair_block: int32 [128, 112], P(('gx', 'gy')), may hold values from 0 to 63, as said below
- crossing: bfloat16 [128, 112, 3, 128, 128], P(('gx', 'gy')), as said below
- kappa: float32 [18], replicated, may hold values from 0.2 to 2
Outputs:
- new_fields: float32 [18, 1024, 1024], P(None, 'gx', 'gy')
- flux_residual: float32 [18, 1024, 1024], P(None, 'gx', 'gy')
The draws below stay inside these ranges and needn't reach their ends.
Inputs may be any that keep to these rules, and one draw needn't show every extreme that they name: `send_block`: entry d * 2 + c of row s is the old row that device s sends in slot c to device d, or -1 where the slot is empty; every slot named by pair_slot is filled, all others are -1. `pair_slot`: in each row the entries are distinct; entry e names source e // 2; each device receives from some one source all 2 of its slots. `pair_block`: every new block of a device is named by at least one of its pairs. `crossing`: volumes are positive.
All inputs are finite; a program needn't handle non-finite values.
Results may differ from the reference program's by a relative error of at most 0.0029.
Values may be sent and summed in bfloat16 or wider, within the bound.
A program may use at most 128 MiB of HBM per device.

```python
import math
import jax
import jax.numpy as jnp
from jax import lax

FIELDS = 18
BLOCK = 128
ROWS = 64
PAIRS = 112
CAP = 2
XCELLS = 1024
YCELLS = 1024
N_GX = 16
N_GY = 8


def routing(key):
    devices = N_GX * N_GY
    pool = devices * CAP
    keys = jax.random.split(key, 5)
    favored = jax.random.randint(keys[0], (devices,), 0, devices)
    scores = jax.random.randint(keys[1], (devices, pool), 0, 2 ** 20)
    entry = jnp.arange(pool, dtype=jnp.int32)
    owner = entry // CAP
    first = owner[None, :] == favored[:, None]
    keyed = jnp.where(first, (entry % CAP)[None, :], pool + scores * pool + entry[None, :])
    keyed = jnp.where(jnp.logical_and(entry[None, :] == pool - 1, jnp.logical_not(first)), CAP, keyed)
    order = jnp.argsort(keyed, axis=1)
    slot_ids = order[:, :PAIRS].astype(jnp.int32)
    ranks = jax.random.randint(keys[2], (devices, ROWS), 0, 2 ** 20) * ROWS + jnp.arange(ROWS, dtype=jnp.int32)[None, :]
    covered = jnp.argsort(ranks, axis=1).astype(jnp.int32)
    extra = jax.random.randint(keys[3], (devices, PAIRS - ROWS), 0, ROWS)
    targets = jnp.concatenate([covered, extra], 1).astype(jnp.int32)
    old_rows = jax.random.randint(keys[4], (devices, PAIRS), 0, ROWS).astype(jnp.int32)
    old_rows = old_rows.at[:, 0].set(ROWS - 1)
    return (slot_ids, targets, old_rows)


def draw_send_block(key, part):
    slot_ids, targets, old_rows = routing(key)
    devices = N_GX * N_GY
    table = jnp.full((devices, devices * CAP), -1, jnp.int32)
    table = table.at[jnp.arange(devices)[:, None], slot_ids].set(old_rows)
    table = table.reshape(devices, devices, CAP).transpose(1, 0, 2)
    return table.reshape(devices, devices * CAP)


def draw_pair_slot(key, part):
    slot_ids, targets, old_rows = routing(key)
    return slot_ids


def draw_pair_block(key, part):
    slot_ids, targets, old_rows = routing(key)
    return targets


def draw_crossing(key, part):
    key = jax.random.fold_in(key, 14)
    keys = jax.random.split(key, 3)
    devices = N_GX * N_GY
    shape = (devices, PAIRS, BLOCK, BLOCK)
    offdiag = jax.random.uniform(keys[0], shape, jnp.float32, 0.0, 2.0 / BLOCK)
    diagonal = jnp.exp(jax.random.uniform(keys[1], (devices, PAIRS, BLOCK), jnp.float32, -0.7, 0.7))
    spread = 0.5
    identity = jnp.eye(BLOCK, dtype=jnp.float32)
    volumes = offdiag * (1.0 - identity) + diagonal[:, :, None, :] * identity
    moments = volumes[:, :, None] * spread * jax.random.normal(keys[2], (devices, PAIRS, 2, BLOCK, BLOCK), jnp.float32)
    return jnp.concatenate([volumes[:, :, None], moments], 2).astype(jnp.bfloat16)


def shard_levels(rng, dims, cuts, low, top_value):
    def one(axis_at, parts):
        draws = jax.random.uniform(jax.random.fold_in(jax.random.fold_in(rng, 6), axis_at), (parts,), jnp.float32, low / len(cuts), top_value / len(cuts))
        return jnp.repeat(jnp.exp(draws), dims[axis_at] // parts).reshape((-1,) + (1,) * (len(dims) - axis_at - 1))

    level = one(*cuts[0])
    for cut in cuts[1:]:
        level = level * one(*cut)
    return level


def bell_draw(key, shape, scale, most, pieces=(), kind=jnp.bfloat16):
    entries = jax.random.normal(key, shape, jnp.float32) * scale
    if len(pieces) > 0:
        entries = shard_levels(key, shape, pieces, -0.22, 0.18) * entries
    return jnp.clip(entries, min=-most, max=most).astype(kind)


def setup_inputs(seed: int = 0) -> dict:
    streams_of = jax.random.split(jax.random.key(seed), 7)
    old_fields = bell_draw(streams_of[0], (FIELDS, XCELLS, YCELLS), 1.0, 6.0, ((1, 16), (2, 8)), jnp.float32)
    send_block = draw_send_block(jax.random.fold_in(streams_of[6], 71), 0)
    pair_slot = draw_pair_slot(jax.random.fold_in(streams_of[6], 71), 0)
    pair_block = draw_pair_block(jax.random.fold_in(streams_of[6], 71), 0)
    crossing = draw_crossing(jax.random.fold_in(streams_of[6], 71), 0)
    kappa = jnp.clip(jnp.exp(jax.random.uniform(streams_of[5], (FIELDS,), jnp.float32, math.log(0.2), math.log(2.0))), 0.2, 2.0)
    return {"old_fields": old_fields, "send_block": send_block, "pair_slot": pair_slot, "pair_block": pair_block, "crossing": crossing, "kappa": kappa}


def minmod(first, second):
    same = first * second > 0.0
    least = jnp.minimum(jnp.abs(first), jnp.abs(second))
    return jnp.where(same, jnp.sign(first) * least, jnp.zeros_like(first))


def shifted(values):
    padded = jnp.pad(values, ((0, 0), (1, 1), (1, 1)), mode="edge")
    return padded[:, :-2, 1:-1], padded[:, 2:, 1:-1], padded[:, 1:-1, :-2], padded[:, 1:-1, 2:]


def reference(old_fields, send_block, pair_slot, pair_block, crossing, kappa):
    upper_row, lower_row, left_col, right_col = shifted(old_fields)
    grad_x = minmod(lower_row - old_fields, old_fields - upper_row)
    grad_y = minmod(right_col - old_fields, old_fields - left_col)
    stacked = jnp.concatenate([old_fields, grad_x, grad_y], 0).astype(jnp.bfloat16)
    devices = N_GX * N_GY
    blocks = stacked.reshape(3 * FIELDS, N_GX, ROWS, N_GY, BLOCK).transpose(1, 3, 2, 0, 4)
    blocks = blocks.reshape(devices, ROWS, 3 * FIELDS, BLOCK)

    def remap(target):
        slot_ids = pair_slot[target]
        source = slot_ids // CAP
        column = target * CAP + slot_ids % CAP
        rows_used = send_block[source, column]
        picked = blocks[source, rows_used].astype(jnp.float32).reshape(PAIRS, 3, FIELDS, BLOCK)
        weights = crossing[target].astype(jnp.float32)
        contrib = jnp.einsum("pkfo,pkon->pfn", picked, weights, precision=lax.Precision.HIGHEST)
        remapped = jax.ops.segment_sum(contrib, pair_block[target], num_segments=ROWS)
        volume = jax.ops.segment_sum(jnp.sum(weights[:, 0], axis=1), pair_block[target], num_segments=ROWS)
        return remapped / volume[:, None, :]

    new_blocks = lax.map(remap, jnp.arange(devices, dtype=jnp.int32))
    new_fields = new_blocks.reshape(N_GX, N_GY, ROWS, FIELDS, BLOCK).transpose(3, 0, 2, 1, 4)
    new_fields = new_fields.reshape(FIELDS, N_GX * ROWS, N_GY * BLOCK)
    upper_row, lower_row, left_col, right_col = shifted(new_fields)
    laplace = upper_row + lower_row + left_col + right_col - 4.0 * new_fields
    return new_fields, kappa[:, None, None] * laplace
```

```python
import functools

import jax
import jax.numpy as jnp
from jax import lax
from jax.experimental import pallas as pl
from jax.experimental.pallas import tpu as pltpu
from jax.sharding import PartitionSpec as P

MESH = pl.DeviceIdType.MESH
F32 = jnp.float32
BF16 = jnp.bfloat16

FIELDS = 18
FULL = 16
ROWS = 64
LANES = 128
PAIRS = 112
CAP = 2
SLAB = 24
VOLUME = 18


def minmod(first, second):
    least = jnp.where(first > 0.0, jnp.minimum(first, second), jnp.maximum(first, second))
    return jnp.where(first * second > 0.0, least, jnp.zeros_like(first))


def iota(shape, axis):
    return lax.broadcasted_iota(jnp.int32, shape, axis)


def loop(count, step, body):
    def outer(n, carry):
        for part in range(step):
            body(n * step + part)
        return carry

    lax.fori_loop(0, count // step, outer, 0)


def kernel(
    nx,
    ny,
    old_hbm,
    crossing_hbm,
    wanted,
    slots,
    blocks,
    kappa,
    new_ref,
    flux_ref,
    u,
    gx,
    gy,
    rest,
    table_u,
    table_g,
    table_lo,
    table_hi,
    send_a,
    send_b,
    recv_a,
    recv_b,
    weights,
    contrib,
    row_out,
    row_in,
    col_out,
    col_in,
    row_out2,
    row_in2,
    col_out2,
    col_in2,
    local_sem,
    halo_send,
    halo_recv,
    halo_send2,
    halo_recv2,
    send_sem,
    recv_sem,
):
    i = lax.axis_index("gx")
    j = lax.axis_index("gy")
    count = nx * ny
    me = i * ny + j

    get_old = pltpu.make_async_copy(old_hbm, u.at[pl.ds(0, FIELDS * ROWS)], local_sem.at[0])
    get_old.start()
    get_weights = pltpu.make_async_copy(crossing_hbm, weights, local_sem.at[1])
    get_weights.start()

    barrier = pltpu.get_barrier_semaphore()

    def greet(k, carry):
        d = lax.rem(me + k, count)
        pl.semaphore_signal(
            barrier, inc=1, device_id=(d // ny, lax.rem(d, ny)), device_id_type=MESH
        )
        return carry

    lax.fori_loop(1, count, greet, 0)

    after_x = (lax.rem(i + 1, nx), j)
    before_x = (lax.rem(i + nx - 1, nx), j)
    after_y = (i, lax.rem(j + 1, ny))
    before_y = (i, lax.rem(j + ny - 1, ny))
    first_x, last_x = i == 0, i == nx - 1
    first_y, last_y = j == 0, j == ny - 1

    lane = iota((ROWS, LANES), 1)
    row = iota((ROWS, LANES), 0)

    def field(ref, f):
        return ref[pl.ds(f * ROWS, ROWS), :]

    zeros = jnp.zeros((ROWS, LANES), F32)
    for f in range(FIELDS, SLAB):
        u[pl.ds(f * ROWS, ROWS), :] = zeros
        gy[pl.ds(f * ROWS, ROWS), :] = zeros
    for f in range(4, 8):
        rest[pl.ds(f * ROWS, ROWS), :] = zeros
    get_old.wait()
    row_out[0] = u[pl.ds(ROWS - 1, SLAB, stride=ROWS), :]
    row_out[1] = u[pl.ds(0, SLAB, stride=ROWS), :]
    head, tail = zeros, zeros
    for f in range(FIELDS):
        cells = field(u, f)
        head = jnp.where(lane == f, pltpu.roll(cells, f, 1) if f else cells, head)
        tail = jnp.where(lane == f, pltpu.roll(cells, f + 1, 1), tail)
    col_out[0] = tail
    col_out[1] = head

    def value_row(r):
        table_u[r] = u[pl.ds(r, FULL, stride=ROWS), :].astype(BF16)

    loop(ROWS, 8, value_row)

    pl.semaphore_wait(barrier, count - 1)

    halo = []
    for n, (source, target, device) in enumerate(
        (
            (row_out.at[0], row_in.at[0], after_x),
            (row_out.at[1], row_in.at[1], before_x),
            (col_out.at[0], col_in.at[0], after_y),
            (col_out.at[1], col_in.at[1], before_y),
        )
    ):
        copy = pltpu.make_async_remote_copy(
            src_ref=source,
            dst_ref=target,
            send_sem=halo_send.at[n],
            recv_sem=halo_recv.at[n],
            device_id=device,
            device_id_type=MESH,
        )
        copy.start()
        halo.append(copy)

    y, z = i // 4, lax.rem(i, 4)
    x, c = j // 2, lax.rem(j, 2)

    def partner(k):
        kc = k // 64
        low = lax.rem(k, 64)
        kx = lax.rem(low, 4)
        ky = lax.rem(low // 4 + kx, 4)
        kz = lax.rem(low // 16 + kx + 2 * ky, 4)
        di = lax.rem(y + ky, 4) * 4 + lax.rem(z + kz, 4)
        dj = lax.rem(x + kx, 4) * 2 + lax.rem(c + kc, 2)
        return di, dj

    def row_of(d, slot):
        return jnp.maximum(wanted[0, d * CAP + slot], 0)

    def pack_a(ref, at, d):
        ref[2 * at] = table_u[row_of(d, 0)]
        ref[2 * at + 1] = table_u[row_of(d, 1)]

    def send_part_a(k, carry):
        di, dj = partner(k)
        d = di * ny + dj
        pack_a(send_a, d, d)
        pltpu.make_async_remote_copy(
            src_ref=send_a.at[pl.ds(2 * d, 2)],
            dst_ref=recv_a.at[pl.ds(2 * me, 2)],
            send_sem=send_sem.at[0],
            recv_sem=recv_sem.at[0],
            device_id=(di, dj),
            device_id_type=MESH,
        ).start()
        return carry

    lax.fori_loop(1, count, send_part_a, 0)
    pack_a(recv_a, me, me)

    for copy in halo:
        copy.wait()
    for f in range(FIELDS):
        cells = field(u, f)
        north = jnp.where(first_x, cells[0:1, :], row_in[0, f : f + 1, :])
        south = jnp.where(last_x, cells[ROWS - 1 :, :], row_in[1, f : f + 1, :])
        upper = jnp.where(row == 0, north, pltpu.roll(cells, 1, 0))
        lower = jnp.where(row == ROWS - 1, south, pltpu.roll(cells, ROWS - 1, 0))
        grad = minmod(lower - cells, cells - upper)
        gx[pl.ds(f * ROWS, ROWS), :] = grad
        west = pltpu.roll(col_in[0], LANES - f, 1) if f else col_in[0]
        east = pltpu.roll(col_in[1], LANES - 1 - f, 1)
        west = jnp.where(first_y, cells, west)
        east = jnp.where(last_y, cells, east)
        left = jnp.where(lane == 0, west, pltpu.roll(cells, 1, 1))
        right = jnp.where(lane == LANES - 1, east, pltpu.roll(cells, LANES - 1, 1))
        gy[pl.ds(f * ROWS, ROWS), :] = minmod(right - cells, cells - left)
        if f >= FULL:
            rest[pl.ds((f - FULL) * ROWS, ROWS), :] = cells
            rest[pl.ds((2 + f - FULL) * ROWS, ROWS), :] = grad

    small_lane = iota((8, LANES), 1)
    small_row = iota((8, LANES), 0)

    def gradient_row(r):
        table_g[r] = gx[pl.ds(r, FULL, stride=ROWS), :].astype(BF16)
        table_lo[r] = rest[pl.ds(r, 8, stride=ROWS), :]
        edges = pltpu.roll(gy[pl.ds(r, 8, stride=ROWS), :], 1, 1)
        middle = pltpu.roll(gy[pl.ds(8 * ROWS + r, 8, stride=ROWS), :], 3, 1)
        last = pltpu.roll(gy[pl.ds(16 * ROWS + r, 8, stride=ROWS), :], 5, 1)
        table_hi[r] = jnp.where(small_lane < 2, edges, jnp.where(small_lane < 4, middle, last))

    loop(ROWS, 8, gradient_row)

    def pack_b(ref, at, d):
        r0, r1 = row_of(d, 0), row_of(d, 1)
        ref[3 * at] = table_g[r0]
        ref[3 * at + 1] = table_g[r1]
        low = jnp.where(small_row < 4, table_lo[r0], pltpu.roll(table_lo[r1], 4, 0))
        high = jnp.where(small_lane < 64, table_hi[r0], pltpu.roll(table_hi[r1], 64, 1))
        ref[3 * at + 2] = jnp.concatenate([low, high], 0).astype(BF16)

    def send_part_b(k, carry):
        di, dj = partner(k)
        d = di * ny + dj
        pack_b(send_b, d, d)
        pltpu.make_async_remote_copy(
            src_ref=send_b.at[pl.ds(3 * d, 3)],
            dst_ref=recv_b.at[pl.ds(3 * me, 3)],
            send_sem=send_sem.at[1],
            recv_sem=recv_sem.at[1],
            device_id=(di, dj),
            device_id_type=MESH,
        ).start()
        return carry

    lax.fori_loop(1, count, send_part_b, 0)
    pack_b(recv_b, me, me)

    get_weights.wait()
    others = count - 1
    for n, (out, landed, tiles) in enumerate(((send_a, recv_a, 2), (send_b, recv_b, 3))):
        whole = pl.ds(0, tiles * others)
        pltpu.make_async_copy(landed.at[whole], landed.at[whole], recv_sem.at[n]).wait()

    def grad_y(cells, west, east):
        lanes = iota(cells.shape, 1)
        step = pltpu.roll(cells, LANES - 1, 1) - cells
        inner = minmod(step, pltpu.roll(step, 1, 1))
        return jnp.where(lanes == 0, west, jnp.where(lanes == LANES - 1, east, inner))

    def product(p):
        e = slots[0, p]
        s = e // 2
        second = lax.rem(e, 2) == 1
        values = recv_a[e]
        grads = recv_b[3 * s + lax.rem(e, 2)]
        mixed = recv_b[3 * s + 2].astype(F32)
        low, high = mixed[0:8], mixed[8:16]
        low = jnp.where(second, pltpu.roll(low, 4, 0), low)
        high = jnp.where(second, pltpu.roll(high, 64, 1), high)
        wide = values.astype(F32)
        parts = []
        for n, cells in enumerate((wide[0:8], wide[8:16], low)):
            ends = pltpu.roll(high, LANES - 1 - 2 * n, 1)
            parts.append(grad_y(cells, ends, ends))
        is_volume = small_row == VOLUME - FULL
        blank = jnp.zeros((8, LANES), F32)
        low_u = jnp.where(is_volume, jnp.ones((8, LANES), F32), low)
        low_g = jnp.where(is_volume, blank, pltpu.roll(low, 6, 0))
        low_y = jnp.where(is_volume, blank, parts[2])
        upper = jnp.concatenate(
            [values, grads, jnp.concatenate(parts[:2], 0).astype(BF16)], 1
        )
        lower = jnp.concatenate([low_u, low_g, low_y], 1).astype(BF16)
        left = jnp.concatenate([upper, lower], 0)
        contrib[pl.ds(pl.multiple_of(p * SLAB, SLAB), SLAB), :] = jnp.dot(
            left, weights[p], preferred_element_type=F32
        )

    loop(PAIRS, 4, product)

    chosen = (iota((ROWS, PAIRS), 0) == blocks[...]).astype(BF16)

    def gathered(f):
        terms = contrib[pl.ds(f, PAIRS, stride=SLAB), :]
        high = terms.astype(BF16)
        low = (terms - high.astype(F32)).astype(BF16)
        return jnp.dot(chosen, high, preferred_element_type=F32) + jnp.dot(
            chosen, low, preferred_element_type=F32
        )

    volume = gathered(VOLUME)
    head, tail = zeros, zeros
    for f in range(FIELDS):
        cells = gathered(f) / volume
        u[pl.ds(f * ROWS, ROWS), :] = cells
        head = jnp.where(lane == f, pltpu.roll(cells, f, 1) if f else cells, head)
        tail = jnp.where(lane == f, pltpu.roll(cells, f + 1, 1), tail)

    blank = jnp.zeros((8, LANES), F32)
    row_out2[0] = jnp.concatenate([u[pl.ds(ROWS - 1, SLAB, stride=ROWS), :], blank], 0).astype(BF16)
    row_out2[1] = jnp.concatenate([u[pl.ds(0, SLAB, stride=ROWS), :], blank], 0).astype(BF16)
    col_out2[0] = tail.astype(BF16)
    col_out2[1] = head.astype(BF16)
    halo = []
    for n, (source, target, device) in enumerate(
        (
            (row_out2.at[0], row_in2.at[0], after_x),
            (row_out2.at[1], row_in2.at[1], before_x),
            (col_out2.at[0], col_in2.at[0], after_y),
            (col_out2.at[1], col_in2.at[1], before_y),
        )
    ):
        copy = pltpu.make_async_remote_copy(
            src_ref=source,
            dst_ref=target,
            send_sem=halo_send2.at[n],
            recv_sem=halo_recv2.at[n],
            device_id=device,
            device_id_type=MESH,
        )
        copy.start()
        halo.append(copy)
    new_ref[...] = u[pl.ds(0, FIELDS * ROWS), :]
    for copy in halo:
        copy.wait()
    norths = row_in2[0].astype(F32)
    souths = row_in2[1].astype(F32)
    wests = col_in2[0].astype(F32)
    easts = col_in2[1].astype(F32)
    for f in range(FIELDS):
        cells = field(u, f)
        north = jnp.where(first_x, cells[0:1, :], norths[f : f + 1, :])
        south = jnp.where(last_x, cells[ROWS - 1 :, :], souths[f : f + 1, :])
        upper = jnp.where(row == 0, north, pltpu.roll(cells, 1, 0))
        lower = jnp.where(row == ROWS - 1, south, pltpu.roll(cells, ROWS - 1, 0))
        west = jnp.where(first_y, cells, pltpu.roll(wests, LANES - f, 1) if f else wests)
        east = jnp.where(last_y, cells, pltpu.roll(easts, LANES - 1 - f, 1))
        left = jnp.where(lane == 0, west, pltpu.roll(cells, 1, 1))
        right = jnp.where(lane == LANES - 1, east, pltpu.roll(cells, LANES - 1, 1))
        flux_ref[pl.ds(f * ROWS, ROWS), :] = kappa[f] * (
            upper + lower + left + right - 4.0 * cells
        )

    for n, (out, landed, tiles) in enumerate(((send_a, recv_a, 2), (send_b, recv_b, 3))):
        whole = pl.ds(0, tiles * others)
        pltpu.make_async_copy(out.at[whole], out.at[whole], send_sem.at[n]).wait()


def shards(nx, ny, old_fields, send_block, pair_slot, pair_block, crossing, kappa):
    shape = old_fields.shape
    count = nx * ny
    flat = (FIELDS * ROWS, LANES)
    padded = (SLAB * ROWS, LANES)
    any_space = pl.BlockSpec(memory_space=pl.ANY)
    smem = pl.BlockSpec(memory_space=pltpu.SMEM)
    vmem = pl.BlockSpec(memory_space=pltpu.VMEM)
    new_fields, flux = pl.pallas_call(
        functools.partial(kernel, nx, ny),
        out_shape=(jax.ShapeDtypeStruct(flat, F32), jax.ShapeDtypeStruct(flat, F32)),
        in_specs=[any_space, any_space, smem, smem, vmem, smem],
        out_specs=(vmem, vmem),
        scratch_shapes=[
            pltpu.VMEM(padded, F32),
            pltpu.VMEM(flat, F32),
            pltpu.VMEM(padded, F32),
            pltpu.VMEM((8 * ROWS, LANES), F32),
            pltpu.VMEM((ROWS, FULL, LANES), BF16),
            pltpu.VMEM((ROWS, FULL, LANES), BF16),
            pltpu.VMEM((ROWS, 8, LANES), F32),
            pltpu.VMEM((ROWS, 8, LANES), F32),
            pltpu.VMEM((2 * count, 16, LANES), BF16),
            pltpu.VMEM((3 * count, 16, LANES), BF16),
            pltpu.VMEM((2 * count, 16, LANES), BF16),
            pltpu.VMEM((3 * count, 16, LANES), BF16),
            pltpu.VMEM((PAIRS, 3 * LANES, LANES), BF16),
            pltpu.VMEM((PAIRS * SLAB, LANES), F32),
            pltpu.VMEM((2, SLAB, LANES), F32),
            pltpu.VMEM((2, SLAB, LANES), F32),
            pltpu.VMEM((2, ROWS, LANES), F32),
            pltpu.VMEM((2, ROWS, LANES), F32),
            pltpu.VMEM((2, 32, LANES), BF16),
            pltpu.VMEM((2, 32, LANES), BF16),
            pltpu.VMEM((2, ROWS, LANES), BF16),
            pltpu.VMEM((2, ROWS, LANES), BF16),
            pltpu.SemaphoreType.DMA((2,)),
            pltpu.SemaphoreType.DMA((4,)),
            pltpu.SemaphoreType.DMA((4,)),
            pltpu.SemaphoreType.DMA((4,)),
            pltpu.SemaphoreType.DMA((4,)),
            pltpu.SemaphoreType.DMA((2,)),
            pltpu.SemaphoreType.DMA((2,)),
        ],
        compiler_params=pltpu.CompilerParams(
            collective_id=0, has_side_effects=True, vmem_limit_bytes=48 * 2**20
        ),
        cost_estimate=pl.CostEstimate(
            flops=2 * PAIRS * 3 * LANES * LANES * SLAB,
            bytes_accessed=12 * 2**20,
            transcendentals=0,
        ),
    )(
        old_fields.reshape(flat),
        crossing.reshape(PAIRS, 3 * LANES, LANES),
        send_block,
        pair_slot,
        pair_block,
        kappa,
    )
    return new_fields.reshape(shape), flux.reshape(shape)


def solution(mesh):
    placed = (
        P(None, "gx", "gy"),
        P(("gx", "gy"), None),
        P(("gx", "gy"), None),
        P(("gx", "gy"), None),
        P(("gx", "gy"), None, None, None, None),
        P(),
    )
    return jax.shard_map(
        functools.partial(shards, mesh.shape["gx"], mesh.shape["gy"]),
        mesh=mesh,
        in_specs=placed,
        out_specs=(P(None, "gx", "gy"), P(None, "gx", "gy")),
        check_vma=False,
    )
```

```python
import functools

import jax
import jax.numpy as jnp
from jax import lax
from jax.experimental import pallas as pl
from jax.experimental.pallas import tpu as pltpu
from jax.sharding import PartitionSpec as P

MESH = pl.DeviceIdType.MESH
F32 = jnp.float32
BF16 = jnp.bfloat16

FIELDS = 18
FULL = 16
ROWS = 64
LANES = 128
PAIRS = 112
CAP = 2
GROUP = 6
SLAB = 24
VOLUME = 18


def chip_offsets():
    groups, seen = [], {(0, 0, 0)}
    for code in range(1, 64):
        offset = (code // 16, code // 4 % 4, code % 4)
        group = []
        for sign in (1, -1):
            for turn in range(3):
                other = tuple(sign * offset[(turn + axis) % 3] % 4 for axis in range(3))
                if other not in seen:
                    seen.add(other)
                    group.append(other)
        if group:
            groups.append(group)
    groups.sort(key=lambda group: -sum(min(step, 4 - step) for step in group[0]))
    codes = [kx + 4 * ky + 16 * kz for group in groups for kx, ky, kz in group]
    return [sum(codes[n + m] * 64**m for m in range(3)) for n in range(0, len(codes), 3)]


ORDER = chip_offsets()


def minmod(first, second):
    least = jnp.where(first > 0.0, jnp.minimum(first, second), jnp.maximum(first, second))
    return jnp.where(first * second > 0.0, least, jnp.zeros_like(first))


def iota(shape, axis):
    return lax.broadcasted_iota(jnp.int32, shape, axis)


def loop(count, step, body):
    def outer(n, carry):
        for part in range(step):
            body(n * step + part)
        return carry

    lax.fori_loop(0, count // step, outer, 0)


def kernel(
    nx,
    ny,
    old_hbm,
    crossing_hbm,
    wanted_hbm,
    slots_hbm,
    blocks_hbm,
    new_ref,
    row_ref,
    col_ref,
    u,
    gx,
    gy,
    rest,
    table_u,
    table_g,
    table_lo,
    table_hi,
    send_a,
    send_b,
    send_c,
    recv_a,
    recv_b,
    recv_c,
    wanted,
    slots,
    blocks,
    weights,
    contrib,
    row_out,
    row_in,
    col_out,
    col_in,
    row_out2,
    row_in2,
    col_out2,
    col_in2,
    local_sem,
    halo_send,
    halo_recv,
    halo_send2,
    halo_recv2,
    send_sem,
    recv_sem,
):
    i = lax.axis_index("gx")
    j = lax.axis_index("gy")
    count = nx * ny
    me = i * ny + j

    get_old = pltpu.make_async_copy(old_hbm, u.at[pl.ds(0, FIELDS * ROWS)], local_sem.at[0])
    get_old.start()
    small = []
    for n, (source, target) in enumerate(
        ((wanted_hbm, wanted), (slots_hbm, slots), (blocks_hbm, blocks))
    ):
        copy = pltpu.make_async_copy(source, target, local_sem.at[2 + n])
        copy.start()
        small.append(copy)
    get_weights = pltpu.make_async_copy(crossing_hbm, weights, local_sem.at[1])
    get_weights.start()

    barrier = pltpu.get_barrier_semaphore()

    def greet(k, carry):
        d = lax.rem(me + k, count)
        pl.semaphore_signal(
            barrier, inc=1, device_id=(d // ny, lax.rem(d, ny)), device_id_type=MESH
        )
        return carry

    lax.fori_loop(1, count, greet, 0)

    after_x = (lax.rem(i + 1, nx), j)
    before_x = (lax.rem(i + nx - 1, nx), j)
    after_y = (i, lax.rem(j + 1, ny))
    before_y = (i, lax.rem(j + ny - 1, ny))
    first_x, last_x = i == 0, i == nx - 1
    first_y, last_y = j == 0, j == ny - 1

    lane = iota((ROWS, LANES), 1)
    row = iota((ROWS, LANES), 0)

    def field(ref, f):
        return ref[pl.ds(f * ROWS, ROWS), :]

    zeros = jnp.zeros((ROWS, LANES), F32)
    for f in range(FIELDS, SLAB):
        u[pl.ds(f * ROWS, ROWS), :] = zeros
        gy[pl.ds(f * ROWS, ROWS), :] = zeros
    for f in range(4, 8):
        rest[pl.ds(f * ROWS, ROWS), :] = zeros
    get_old.wait()
    row_out[0] = u[pl.ds(ROWS - 1, SLAB, stride=ROWS), :]
    row_out[1] = u[pl.ds(0, SLAB, stride=ROWS), :]
    head, tail = zeros, zeros
    for f in range(FIELDS):
        cells = field(u, f)
        head = jnp.where(lane == f, pltpu.roll(cells, f, 1) if f else cells, head)
        tail = jnp.where(lane == f, pltpu.roll(cells, f + 1, 1), tail)
    col_out[0] = tail
    col_out[1] = head

    def value_row(r):
        table_u[r] = u[pl.ds(r, FULL, stride=ROWS), :].astype(BF16)

    loop(ROWS, 8, value_row)

    pl.semaphore_wait(barrier, count - 1)

    halo = []
    for n, (source, target, device) in enumerate(
        (
            (row_out.at[0], row_in.at[0], after_x),
            (row_out.at[1], row_in.at[1], before_x),
            (col_out.at[0], col_in.at[0], after_y),
            (col_out.at[1], col_in.at[1], before_y),
        )
    ):
        copy = pltpu.make_async_remote_copy(
            src_ref=source,
            dst_ref=target,
            send_sem=halo_send.at[n],
            recv_sem=halo_recv.at[n],
            device_id=device,
            device_id_type=MESH,
        )
        copy.start()
        halo.append(copy)

    y, z = i // 4, lax.rem(i, 4)
    x, c = j // 2, lax.rem(j, 2)

    def to_partners(body):
        def visit(kx, ky, kz, kc):
            di = lax.rem(y + ky, 4) * 4 + lax.rem(z + kz, 4)
            dj = lax.rem(x + kx, 4) * 2 + lax.rem(c + kc, 2)
            body(di * ny + dj, (di, dj))

        def some(n, carry):
            kc = n // len(ORDER)
            at = lax.rem(n, len(ORDER))
            word = jnp.int32(ORDER[0])
            for m in range(1, len(ORDER)):
                word = jnp.where(at == m, jnp.int32(ORDER[m]), word)
            for part in range(3):
                code = word // 64**part
                visit(lax.rem(code, 4), lax.rem(code // 4, 4), lax.rem(code // 16, 4), kc)
            return carry

        lax.fori_loop(0, len(ORDER), some, 0)
        visit(0, 0, 0, 1)
        lax.fori_loop(len(ORDER), 2 * len(ORDER), some, 0)

    def row_of(d, slot):
        return jnp.maximum(wanted[0, d * CAP + slot], 0)

    def pack_a(ref, at, d):
        ref[2 * at] = table_u[row_of(d, 0)]
        ref[2 * at + 1] = table_u[row_of(d, 1)]

    def send(n, tiles, pack, out, landed):
        def one(d, device):
            pack(out, d, d)
            pltpu.make_async_remote_copy(
                src_ref=out.at[pl.ds(tiles * d, tiles)],
                dst_ref=landed.at[pl.ds(tiles * me, tiles)],
                send_sem=send_sem.at[n],
                recv_sem=recv_sem.at[n],
                device_id=device,
                device_id_type=MESH,
            ).start()

        to_partners(one)
        pack(landed, me, me)

    small[0].wait()
    send(0, 2, pack_a, send_a, recv_a)

    for copy in halo:
        copy.wait()
    for f in range(FIELDS):
        cells = field(u, f)
        north = jnp.where(first_x, cells[0:1, :], row_in[0, f : f + 1, :])
        south = jnp.where(last_x, cells[ROWS - 1 :, :], row_in[1, f : f + 1, :])
        upper = jnp.where(row == 0, north, pltpu.roll(cells, 1, 0))
        lower = jnp.where(row == ROWS - 1, south, pltpu.roll(cells, ROWS - 1, 0))
        grad = minmod(lower - cells, cells - upper)
        gx[pl.ds(f * ROWS, ROWS), :] = grad
        west = pltpu.roll(col_in[0], LANES - f, 1) if f else col_in[0]
        east = pltpu.roll(col_in[1], LANES - 1 - f, 1)
        west = jnp.where(first_y, cells, west)
        east = jnp.where(last_y, cells, east)
        left = jnp.where(lane == 0, west, pltpu.roll(cells, 1, 1))
        right = jnp.where(lane == LANES - 1, east, pltpu.roll(cells, LANES - 1, 1))
        gy[pl.ds(f * ROWS, ROWS), :] = minmod(right - cells, cells - left)
        if f >= FULL:
            rest[pl.ds((f - FULL) * ROWS, ROWS), :] = cells
            rest[pl.ds((2 + f - FULL) * ROWS, ROWS), :] = grad

    small_lane = iota((8, LANES), 1)
    small_row = iota((8, LANES), 0)

    def gradient_row(r):
        table_g[r] = gx[pl.ds(r, FULL, stride=ROWS), :].astype(BF16)
        table_lo[r] = rest[pl.ds(r, 8, stride=ROWS), :]
        edges = pltpu.roll(gy[pl.ds(r, 8, stride=ROWS), :], 1, 1)
        middle = pltpu.roll(gy[pl.ds(8 * ROWS + r, 8, stride=ROWS), :], 3, 1)
        last = pltpu.roll(gy[pl.ds(16 * ROWS + r, 8, stride=ROWS), :], 5, 1)
        table_hi[r] = jnp.where(small_lane < 2, edges, jnp.where(small_lane < 4, middle, last))

    loop(ROWS, 8, gradient_row)

    def pack_c(ref, at, d):
        r0, r1 = row_of(d, 0), row_of(d, 1)
        low = jnp.where(small_row < 4, table_lo[r0], pltpu.roll(table_lo[r1], 4, 0))
        high = jnp.where(small_lane < 64, table_hi[r0], pltpu.roll(table_hi[r1], 64, 1))
        ref[at] = jnp.concatenate([low, high], 0).astype(BF16)

    send(1, 1, pack_c, send_c, recv_c)

    def pack_b(ref, at, d):
        ref[2 * at] = table_g[row_of(d, 0)]
        ref[2 * at + 1] = table_g[row_of(d, 1)]

    send(2, 2, pack_b, send_b, recv_b)

    for copy in small[1:]:
        copy.wait()
    get_weights.wait()
    messages = ((send_a, recv_a, 2), (send_c, recv_c, 1), (send_b, recv_b, 2))

    def landed_whole(n):
        _, landed, tiles = messages[n]
        whole = pl.ds(0, tiles * (count - 1))
        pltpu.make_async_copy(landed.at[whole], landed.at[whole], recv_sem.at[n]).wait()

    landed_whole(0)
    landed_whole(1)

    def grad_y(cells, west, east):
        lanes = iota(cells.shape, 1)
        step = pltpu.roll(cells, LANES - 1, 1) - cells
        inner = minmod(step, pltpu.roll(step, 1, 1))
        return jnp.where(lanes == 0, west, jnp.where(lanes == LANES - 1, east, inner))

    is_volume = small_row == VOLUME - FULL
    ones = jnp.ones((8, LANES), F32)
    blank = jnp.zeros((8, LANES), F32)
    none = jnp.zeros((FULL, LANES), BF16)

    def first_terms(p):
        e = slots[0, p]
        second = lax.rem(e, 2) == 1
        values = recv_a[e]
        mixed = recv_c[e // 2].astype(F32)
        low, high = mixed[0:8], mixed[8:16]
        low = jnp.where(second, pltpu.roll(low, 4, 0), low)
        high = jnp.where(second, pltpu.roll(high, 64, 1), high)
        wide = values.astype(F32)
        parts = []
        for n, cells in enumerate((wide[0:8], wide[8:16], low)):
            ends = pltpu.roll(high, LANES - 1 - 2 * n, 1)
            parts.append(grad_y(cells, ends, ends))
        low_u = jnp.where(is_volume, ones, low)
        low_g = jnp.where(is_volume, blank, pltpu.roll(low, 6, 0))
        low_y = jnp.where(is_volume, blank, parts[2])
        upper = jnp.concatenate([values, none, jnp.concatenate(parts[:2], 0).astype(BF16)], 1)
        lower = jnp.concatenate([low_u, low_g, low_y], 1).astype(BF16)
        return jnp.concatenate([upper, lower], 0)

    def slab(p, size):
        return pl.ds(pl.multiple_of(p * SLAB, SLAB), size)

    def first_product(q):
        p = 2 * q
        left = jnp.concatenate([first_terms(p), first_terms(p + 1)], 0)
        right = jnp.concatenate([weights[p], weights[p + 1]], 1)
        both = jnp.dot(left, right, preferred_element_type=F32)
        contrib[slab(p, SLAB), :] = both[:SLAB, :LANES]
        contrib[slab(p + 1, SLAB), :] = both[SLAB:, LANES:]

    loop(PAIRS // 2, 4, first_product)

    landed_whole(2)

    def second_product(q):
        p = 2 * q
        left = jnp.concatenate([recv_b[slots[0, p]], recv_b[slots[0, p + 1]]], 0)
        middle = pl.ds(LANES, LANES)
        right = jnp.concatenate([weights[p, middle, :], weights[p + 1, middle, :]], 1)
        both = jnp.dot(left, right, preferred_element_type=F32)
        contrib[slab(p, FULL), :] += both[:FULL, :LANES]
        contrib[slab(p + 1, FULL), :] += both[FULL:, LANES:]

    loop(PAIRS // 2, 14, second_product)

    chosen = (iota((ROWS, PAIRS), 0) == blocks[...]).astype(BF16)

    def gathered(f):
        terms = contrib[pl.ds(f, PAIRS, stride=SLAB), :]
        high = terms.astype(BF16)
        low = (terms - high.astype(F32)).astype(BF16)
        return jnp.dot(chosen, high, preferred_element_type=F32) + jnp.dot(
            chosen, low, preferred_element_type=F32
        )

    volume = gathered(VOLUME)
    head, tail = zeros, zeros
    for f in range(FIELDS):
        cells = gathered(f) / volume
        u[pl.ds(f * ROWS, ROWS), :] = cells
        head = jnp.where(lane == f, pltpu.roll(cells, f, 1) if f else cells, head)
        tail = jnp.where(lane == f, pltpu.roll(cells, f + 1, 1), tail)

    row_out2[0] = jnp.concatenate([u[pl.ds(ROWS - 1, SLAB, stride=ROWS), :], blank], 0).astype(BF16)
    row_out2[1] = jnp.concatenate([u[pl.ds(0, SLAB, stride=ROWS), :], blank], 0).astype(BF16)
    col_out2[0] = tail.astype(BF16)
    col_out2[1] = head.astype(BF16)
    halo = []
    for n, (source, target, device) in enumerate(
        (
            (row_out2.at[0], row_in2.at[0], after_x),
            (row_out2.at[1], row_in2.at[1], before_x),
            (col_out2.at[0], col_in2.at[0], after_y),
            (col_out2.at[1], col_in2.at[1], before_y),
        )
    ):
        copy = pltpu.make_async_remote_copy(
            src_ref=source,
            dst_ref=target,
            send_sem=halo_send2.at[n],
            recv_sem=halo_recv2.at[n],
            device_id=device,
            device_id_type=MESH,
        )
        copy.start()
        halo.append(copy)
    new_ref[...] = u[pl.ds(0, FIELDS * ROWS), :]
    for copy in halo:
        copy.wait()
    row_ref[...] = row_in2[...]
    col_ref[...] = col_in2[...]
    for n, (out, _, tiles) in enumerate(messages):
        whole = pl.ds(0, tiles * (count - 1))
        pltpu.make_async_copy(out.at[whole], out.at[whole], send_sem.at[n]).wait()


def finish(nx, ny, cells_ref, row_ref, col_ref, kappa_hbm, new_ref, flux_ref, flux, kappa, sem):
    i = lax.axis_index("gx")
    j = lax.axis_index("gy")
    get_kappa = pltpu.make_async_copy(kappa_hbm, kappa, sem.at[0])
    get_kappa.start()
    put_new = pltpu.make_async_copy(cells_ref, new_ref, sem.at[1])
    put_new.start()
    first_x, last_x = i == 0, i == nx - 1
    first_y, last_y = j == 0, j == ny - 1
    lane = iota((ROWS, LANES), 1)
    row = iota((ROWS, LANES), 0)
    norths = row_ref[0].astype(F32)
    souths = row_ref[1].astype(F32)
    wests = col_ref[0].astype(F32)
    easts = col_ref[1].astype(F32)
    get_kappa.wait()
    puts = []
    for f in range(FIELDS):
        here = pl.ds(f * ROWS, ROWS)
        cells = cells_ref[here, :]
        north = jnp.where(first_x, cells[0:1, :], norths[f : f + 1, :])
        south = jnp.where(last_x, cells[ROWS - 1 :, :], souths[f : f + 1, :])
        upper = jnp.where(row == 0, north, pltpu.roll(cells, 1, 0))
        lower = jnp.where(row == ROWS - 1, south, pltpu.roll(cells, ROWS - 1, 0))
        west = jnp.where(first_y, cells, pltpu.roll(wests, LANES - f, 1) if f else wests)
        east = jnp.where(last_y, cells, pltpu.roll(easts, LANES - 1 - f, 1))
        left = jnp.where(lane == 0, west, pltpu.roll(cells, 1, 1))
        right = jnp.where(lane == LANES - 1, east, pltpu.roll(cells, LANES - 1, 1))
        flux[here, :] = kappa[f] * (upper + lower + left + right - 4.0 * cells)
        if f % GROUP == GROUP - 1:
            part = pl.ds((f + 1 - GROUP) * ROWS, GROUP * ROWS)
            put = pltpu.make_async_copy(flux.at[part], flux_ref.at[part], sem.at[2 + f // GROUP])
            put.start()
            puts.append(put)
    for put in [put_new] + puts:
        put.wait()


def shards(nx, ny, old_fields, send_block, pair_slot, pair_block, crossing, kappa):
    shape = old_fields.shape
    count = nx * ny
    flat = (FIELDS * ROWS, LANES)
    padded = (SLAB * ROWS, LANES)
    hbm = pl.BlockSpec(memory_space=pltpu.HBM)
    vmem = pl.BlockSpec(memory_space=pltpu.VMEM)
    in_hbm = lambda array: pltpu.with_memory_space_constraint(array, pltpu.HBM)
    cells, edge_rows, edge_cols = pl.pallas_call(
        functools.partial(kernel, nx, ny),
        out_shape=(
            jax.ShapeDtypeStruct(flat, F32),
            jax.ShapeDtypeStruct((2, 32, LANES), BF16),
            jax.ShapeDtypeStruct((2, ROWS, LANES), BF16),
        ),
        in_specs=[hbm] * 5,
        out_specs=(vmem,) * 3,
        scratch_shapes=[
            pltpu.VMEM(padded, F32),
            pltpu.VMEM(flat, F32),
            pltpu.VMEM(padded, F32),
            pltpu.VMEM((8 * ROWS, LANES), F32),
            pltpu.VMEM((ROWS, FULL, LANES), BF16),
            pltpu.VMEM((ROWS, FULL, LANES), BF16),
            pltpu.VMEM((ROWS, 8, LANES), F32),
            pltpu.VMEM((ROWS, 8, LANES), F32),
            pltpu.VMEM((2 * count, 16, LANES), BF16),
            pltpu.VMEM((2 * count, 16, LANES), BF16),
            pltpu.VMEM((count, 16, LANES), BF16),
            pltpu.VMEM((2 * count, 16, LANES), BF16),
            pltpu.VMEM((2 * count, 16, LANES), BF16),
            pltpu.VMEM((count, 16, LANES), BF16),
            pltpu.SMEM((1, CAP * count), jnp.int32),
            pltpu.SMEM((1, PAIRS), jnp.int32),
            pltpu.VMEM((1, PAIRS), jnp.int32),
            pltpu.VMEM((PAIRS, 3 * LANES, LANES), BF16),
            pltpu.VMEM((PAIRS * SLAB, LANES), F32),
            pltpu.VMEM((2, SLAB, LANES), F32),
            pltpu.VMEM((2, SLAB, LANES), F32),
            pltpu.VMEM((2, ROWS, LANES), F32),
            pltpu.VMEM((2, ROWS, LANES), F32),
            pltpu.VMEM((2, 32, LANES), BF16),
            pltpu.VMEM((2, 32, LANES), BF16),
            pltpu.VMEM((2, ROWS, LANES), BF16),
            pltpu.VMEM((2, ROWS, LANES), BF16),
            pltpu.SemaphoreType.DMA((5,)),
            pltpu.SemaphoreType.DMA((4,)),
            pltpu.SemaphoreType.DMA((4,)),
            pltpu.SemaphoreType.DMA((4,)),
            pltpu.SemaphoreType.DMA((4,)),
            pltpu.SemaphoreType.DMA((3,)),
            pltpu.SemaphoreType.DMA((3,)),
        ],
        compiler_params=pltpu.CompilerParams(
            collective_id=0, has_side_effects=True, vmem_limit_bytes=48 * 2**20
        ),
        cost_estimate=pl.CostEstimate(
            flops=2 * PAIRS * 3 * LANES * LANES * SLAB,
            bytes_accessed=12 * 2**20,
            transcendentals=0,
        ),
    )(
        in_hbm(old_fields.reshape(flat)),
        in_hbm(crossing.reshape(PAIRS, 3 * LANES, LANES)),
        in_hbm(send_block),
        in_hbm(pair_slot),
        in_hbm(pair_block),
    )
    new_fields, flux = pl.pallas_call(
        functools.partial(finish, nx, ny),
        out_shape=(jax.ShapeDtypeStruct(flat, F32), jax.ShapeDtypeStruct(flat, F32)),
        in_specs=[vmem] * 3 + [hbm],
        out_specs=(hbm, hbm),
        scratch_shapes=[
            pltpu.VMEM(flat, F32),
            pltpu.SMEM((FIELDS,), F32),
            pltpu.SemaphoreType.DMA((2 + FIELDS // GROUP,)),
        ],
        compiler_params=pltpu.CompilerParams(vmem_limit_bytes=4 * 2**20),
    )(cells, edge_rows, edge_cols, in_hbm(kappa))
    return new_fields.reshape(shape), flux.reshape(shape)


def solution(mesh):
    placed = (
        P(None, "gx", "gy"),
        P(("gx", "gy"), None),
        P(("gx", "gy"), None),
        P(("gx", "gy"), None),
        P(("gx", "gy"), None, None, None, None),
        P(),
    )
    return jax.shard_map(
        functools.partial(shards, mesh.shape["gx"], mesh.shape["gy"]),
        mesh=mesh,
        in_specs=placed,
        out_specs=(P(None, "gx", "gy"), P(None, "gx", "gy")),
        check_vma=False,
    )
```

```python
import functools

import jax
import jax.numpy as jnp
from jax import lax
from jax.experimental import pallas as pl
from jax.experimental.pallas import tpu as pltpu
from jax.sharding import PartitionSpec as P

MESH = pl.DeviceIdType.MESH
F32 = jnp.float32
BF16 = jnp.bfloat16

FIELDS = 18
FULL = 16
ROWS = 64
LANES = 128
PAIRS = 112
CAP = 2
SLAB = 24
VOLUME = 18


def chip_offsets():
    groups, seen = [], {(0, 0, 0)}
    for code in range(1, 64):
        offset = (code // 16, code // 4 % 4, code % 4)
        group = []
        for sign in (1, -1):
            for turn in range(3):
                other = tuple(sign * offset[(turn + axis) % 3] % 4 for axis in range(3))
                if other not in seen:
                    seen.add(other)
                    group.append(other)
        if group:
            groups.append(group)
    groups.sort(key=lambda group: -sum(min(step, 4 - step) for step in group[0]))
    codes = [kx + 4 * ky + 16 * kz for group in groups for kx, ky, kz in group]
    return [sum(codes[n + m] * 64**m for m in range(3)) for n in range(0, len(codes), 3)]


ORDER = chip_offsets()


def minmod(first, second):
    least = jnp.where(first > 0.0, jnp.minimum(first, second), jnp.maximum(first, second))
    return jnp.where(first * second > 0.0, least, jnp.zeros_like(first))


def iota(shape, axis):
    return lax.broadcasted_iota(jnp.int32, shape, axis)


def loop(count, step, body):
    def outer(n, carry):
        for part in range(step):
            body(n * step + part)
        return carry

    lax.fori_loop(0, count // step, outer, 0)


def kernel(
    nx,
    ny,
    old_hbm,
    crossing_hbm,
    wanted_hbm,
    slots_hbm,
    blocks_hbm,
    kappa_hbm,
    new_ref,
    flux_ref,
    u,
    gx,
    inner,
    rest,
    table_u,
    table_g,
    table_lo,
    table_e,
    send_a,
    send_b,
    send_c,
    send_e,
    recv_a,
    recv_b,
    recv_c,
    recv_e,
    edges_in,
    edge_tiles,
    wanted,
    slots,
    blocks,
    kappa,
    weights,
    contrib,
    volume,
    row_out,
    row_in,
    col_out,
    col_in,
    row_out2,
    row_in2,
    col_out2,
    col_in2,
    local_sem,
    halo_send,
    halo_recv,
    halo_send2,
    halo_recv2,
    send_sem,
    recv_sem,
):
    i = lax.axis_index("gx")
    j = lax.axis_index("gy")
    count = nx * ny
    me = i * ny + j

    get_old = pltpu.make_async_copy(old_hbm, u.at[pl.ds(0, FIELDS * ROWS)], local_sem.at[0])
    get_old.start()
    small = []
    for n, (source, target) in enumerate(
        ((wanted_hbm, wanted), (slots_hbm, slots), (blocks_hbm, blocks), (kappa_hbm, kappa))
    ):
        copy = pltpu.make_async_copy(source, target, local_sem.at[2 + n])
        copy.start()
        small.append(copy)
    get_weights = pltpu.make_async_copy(crossing_hbm, weights, local_sem.at[1])
    get_weights.start()

    barrier = pltpu.get_barrier_semaphore()

    def greet(k, carry):
        for core in range(2):
            di = lax.rem(i // 4 + 2 + k // 4, 4) * 4 + lax.rem(i + 2 + k, 4)
            dj = lax.rem(lax.rem(j, 2) + core, 2)
            for step in range(4):
                signal(di, lax.rem(j // 2 + 2 + step, 4) * 2 + dj)
        return carry

    def signal(di, dj):
        @pl.when(di * ny + dj != me)
        def _():
            pl.semaphore_signal(barrier, inc=1, device_id=(di, dj), device_id_type=MESH)

    lax.fori_loop(0, nx, greet, 0)

    after_x = (lax.rem(i + 1, nx), j)
    before_x = (lax.rem(i + nx - 1, nx), j)
    after_y = (i, lax.rem(j + 1, ny))
    before_y = (i, lax.rem(j + ny - 1, ny))
    first_x, last_x = i == 0, i == nx - 1
    first_y, last_y = j == 0, j == ny - 1

    lane = iota((ROWS, LANES), 1)
    row = iota((ROWS, LANES), 0)

    def field(ref, f):
        return ref[pl.ds(f * ROWS, ROWS), :]

    zeros = jnp.zeros((ROWS, LANES), F32)
    for f in range(FIELDS, SLAB):
        u[pl.ds(f * ROWS, ROWS), :] = zeros
    for f in range(4, 8):
        rest[pl.ds(f * ROWS, ROWS), :] = zeros
    get_old.wait()
    row_out[0] = u[pl.ds(ROWS - 1, SLAB, stride=ROWS), :]
    row_out[1] = u[pl.ds(0, SLAB, stride=ROWS), :]
    columns = [zeros] * 4
    for f in range(FIELDS):
        cells = field(u, f)
        for n, back in enumerate((0, 1, LANES - 2, LANES - 1)):
            shift = (f - back) % LANES
            moved = pltpu.roll(cells, shift, 1) if shift else cells
            columns[n] = jnp.where(lane == f, moved, columns[n])
    col_out[0] = columns[3]
    col_out[1] = columns[0]
    inner[0] = columns[1]
    inner[1] = columns[2]

    def value_row(r):
        table_u[r] = u[pl.ds(r, FULL, stride=ROWS), :].astype(BF16)

    loop(ROWS, 8, value_row)

    pl.semaphore_wait(barrier, count - 1)

    def exchange(sources, targets, sends, receives):
        copies = []
        for n, device in enumerate((after_x, before_x, after_y, before_y)):
            copy = pltpu.make_async_remote_copy(
                src_ref=sources[n],
                dst_ref=targets[n],
                send_sem=sends.at[n],
                recv_sem=receives.at[n],
                device_id=device,
                device_id_type=MESH,
            )
            pl.when(jnp.logical_not((last_x, first_x, last_y, first_y)[n]))(copy.start)
            copies.append(copy)
        return copies

    def exchanged(copies):
        for n, copy in enumerate(copies):
            pl.when(jnp.logical_not((last_x, first_x, last_y, first_y)[n]))(copy.wait_send)
            pl.when(jnp.logical_not((first_x, last_x, first_y, last_y)[n]))(copy.wait_recv)

    halo = exchange(
        (row_out.at[0], row_out.at[1], col_out.at[0], col_out.at[1]),
        (row_in.at[0], row_in.at[1], col_in.at[0], col_in.at[1]),
        halo_send,
        halo_recv,
    )

    y, z = i // 4, lax.rem(i, 4)
    x, c = j // 2, lax.rem(j, 2)

    def to_partners(body):
        def visit(kx, ky, kz, kc):
            di = lax.rem(y + ky, 4) * 4 + lax.rem(z + kz, 4)
            dj = lax.rem(x + kx, 4) * 2 + lax.rem(c + kc, 2)
            body(di * ny + dj, (di, dj))

        def some(n, carry):
            kc = n // len(ORDER)
            at = lax.rem(n, len(ORDER))
            word = jnp.int32(ORDER[0])
            for m in range(1, len(ORDER)):
                word = jnp.where(at == m, jnp.int32(ORDER[m]), word)
            for part in range(3):
                code = word // 64**part
                visit(lax.rem(code, 4), lax.rem(code // 4, 4), lax.rem(code // 16, 4), kc)
            return carry

        lax.fori_loop(0, len(ORDER), some, 0)
        visit(0, 0, 0, 1)
        lax.fori_loop(len(ORDER), 2 * len(ORDER), some, 0)

    def row_of(d, slot):
        return jnp.maximum(wanted[0, d * CAP + slot], 0)

    def pack_a(ref, at, d):
        ref[2 * at] = table_u[row_of(d, 0)]
        ref[2 * at + 1] = table_u[row_of(d, 1)]

    def send(*parts):
        def one(d, device):
            for n, tiles, pack, out, landed in parts:
                pack(out, d, d)
                pltpu.make_async_remote_copy(
                    src_ref=out.at[pl.ds(tiles * d, tiles)],
                    dst_ref=landed.at[pl.ds(tiles * me, tiles)],
                    send_sem=send_sem.at[n],
                    recv_sem=recv_sem.at[n],
                    device_id=device,
                    device_id_type=MESH,
                ).start()

        to_partners(one)
        for n, tiles, pack, out, landed in parts:
            pack(landed, me, me)

    small[0].wait()
    send((0, 2, pack_a, send_a, recv_a))

    exchanged(halo)
    for f in range(FIELDS):
        cells = field(u, f)
        north = jnp.where(first_x, cells[0:1, :], row_in[0, f : f + 1, :])
        south = jnp.where(last_x, cells[ROWS - 1 :, :], row_in[1, f : f + 1, :])
        upper = jnp.where(row == 0, north, pltpu.roll(cells, 1, 0))
        lower = jnp.where(row == ROWS - 1, south, pltpu.roll(cells, ROWS - 1, 0))
        grad = minmod(lower - cells, cells - upper)
        gx[pl.ds(f * ROWS, ROWS), :] = grad
        if f >= FULL:
            rest[pl.ds((f - FULL) * ROWS, ROWS), :] = cells
            rest[pl.ds((2 + f - FULL) * ROWS, ROWS), :] = grad

    head, tail = col_out[1], col_out[0]
    west = jnp.where(first_y, head, col_in[0])
    east = jnp.where(last_y, tail, col_in[1])
    edges = minmod(inner[0] - head, head - west)
    edges = jnp.where(
        lane < SLAB, edges, pltpu.roll(minmod(east - tail, tail - inner[1]), SLAB, 1)
    )
    edges = jnp.where(lane < 2 * SLAB, edges, 0.0)
    table_e[0] = edges
    table_e[1] = pltpu.roll(edges, 64, 1)

    small_lane = iota((8, LANES), 1)
    small_row = iota((8, LANES), 0)

    def gradient_row(r):
        table_g[r] = gx[pl.ds(r, FULL, stride=ROWS), :].astype(BF16)
        table_lo[r] = rest[pl.ds(r, 8, stride=ROWS), :]

    loop(ROWS, 8, gradient_row)

    def pack_c(ref, at, d):
        low = jnp.where(
            small_row < 4, table_lo[row_of(d, 0)], pltpu.roll(table_lo[row_of(d, 1)], 4, 0)
        )
        ref[at] = low.astype(BF16)

    def pack_e(ref, at, d):
        ref[at] = table_e[0, pl.ds(row_of(d, 0), 1), :] + table_e[1, pl.ds(row_of(d, 1), 1), :]

    send((1, 1, pack_c, send_c, recv_c), (3, 1, pack_e, send_e, recv_e))

    def pack_b(ref, at, d):
        ref[2 * at] = table_g[row_of(d, 0)]
        ref[2 * at + 1] = table_g[row_of(d, 1)]

    send((2, 2, pack_b, send_b, recv_b))

    for copy in small[1:]:
        copy.wait()
    get_weights.wait()
    messages = (
        (send_a, recv_a, 2),
        (send_c, recv_c, 1),
        (send_b, recv_b, 2),
        (send_e, recv_e, 1),
    )

    def landed_whole(n):
        _, landed, tiles = messages[n]
        whole = pl.ds(0, tiles * (count - 1))
        pltpu.make_async_copy(landed.at[whole], landed.at[whole], recv_sem.at[n]).wait()

    landed_whole(0)
    landed_whole(1)
    landed_whole(3)

    def edge_row(source):
        edges_in[pl.ds(source, 1), :] = recv_e[source]

    loop(count, 8, edge_row)
    turned = edges_in[...].T
    even = lax.rem(iota((SLAB, LANES), 1), 2) == 0
    for slot in range(CAP):
        west = turned[64 * slot : 64 * slot + SLAB]
        east = pltpu.roll(turned[64 * slot + SLAB : 64 * slot + 2 * SLAB], LANES - 1, 1)
        edges_in[pl.ds(slot * SLAB, SLAB), :] = jnp.where(even, west, east)
        edges_in[pl.ds((CAP + slot) * SLAB, SLAB), :] = jnp.where(even, east, west)

    def edge_tile(half):
        for odd in range(2):
            source = 2 * half + odd
            for slot in range(CAP):
                at = edges_in[pl.ds((CAP * odd + slot) * SLAB, SLAB), :]
                edge_tiles[CAP * source + slot] = pltpu.roll(at, LANES - source, 1)

    loop(count // 2, 4, edge_tile)

    def grad_y(cells, ends):
        lanes = iota(cells.shape, 1)
        step = pltpu.roll(cells, LANES - 1, 1) - cells
        inner = minmod(step, pltpu.roll(step, 1, 1))
        return jnp.where(jnp.logical_or(lanes == 0, lanes == LANES - 1), ends, inner)

    is_volume = small_row == VOLUME - FULL
    ones = jnp.ones((8, LANES), F32)
    blank = jnp.zeros((8, LANES), F32)
    none = jnp.zeros((FULL, LANES), BF16)

    def first_terms(p):
        e = slots[0, p]
        second = lax.rem(e, 2) == 1
        values = recv_a[e]
        low = recv_c[e // 2].astype(F32)
        low = jnp.where(second, pltpu.roll(low, 4, 0), low)
        wide = values.astype(F32)
        ends = edge_tiles[e]
        parts = [
            grad_y(cells, ends[8 * n : 8 * n + 8])
            for n, cells in enumerate((wide[0:8], wide[8:16], low))
        ]
        low_u = jnp.where(is_volume, ones, low)
        low_g = jnp.where(is_volume, blank, pltpu.roll(low, 6, 0))
        low_y = jnp.where(is_volume, blank, parts[2])
        upper = jnp.concatenate([values, none, jnp.concatenate(parts[:2], 0).astype(BF16)], 1)
        lower = jnp.concatenate([low_u, low_g, low_y], 1).astype(BF16)
        return jnp.concatenate([upper, lower], 0)

    def slab(p, size):
        return pl.ds(pl.multiple_of(p * SLAB, SLAB), size)

    def first_product(q):
        p = 2 * q
        left = jnp.concatenate([first_terms(p), first_terms(p + 1)], 0)
        right = jnp.concatenate([weights[p], weights[p + 1]], 1)
        both = jnp.dot(left, right, preferred_element_type=F32)
        contrib[slab(p, SLAB), :] = both[:SLAB, :LANES]
        contrib[slab(p + 1, SLAB), :] = both[SLAB:, LANES:]

    loop(PAIRS // 2, 7, first_product)

    chosen = (iota((ROWS, PAIRS), 0) == blocks[...]).astype(BF16)

    def gathered(f):
        terms = contrib[pl.ds(f, PAIRS, stride=SLAB), :]
        high = terms.astype(BF16)
        low = (terms - high.astype(F32)).astype(BF16)
        return jnp.dot(chosen, high, preferred_element_type=F32) + jnp.dot(
            chosen, low, preferred_element_type=F32
        )

    volume[...] = gathered(VOLUME)
    for f in range(FIELDS):
        u[pl.ds(f * ROWS, ROWS), :] = gathered(f)

    landed_whole(2)

    def second_product(q):
        p = 2 * q
        left = jnp.concatenate([recv_b[slots[0, p]], recv_b[slots[0, p + 1]]], 0)
        middle = pl.ds(LANES, LANES)
        right = jnp.concatenate([weights[p, middle, :], weights[p + 1, middle, :]], 1)
        both = jnp.dot(left, right, preferred_element_type=F32)
        contrib[slab(p, FULL), :] = both[:FULL, :LANES]
        contrib[slab(p + 1, FULL), :] = both[FULL:, LANES:]

    loop(PAIRS // 2, 14, second_product)

    head, tail = zeros, zeros
    for f in range(FIELDS):
        cells = field(u, f)
        if f < FULL:
            cells = cells + gathered(f)
        cells = cells / volume[...]
        u[pl.ds(f * ROWS, ROWS), :] = cells
        head = jnp.where(lane == 2 * f, pltpu.roll(cells, 2 * f, 1) if f else cells, head)
        tail = jnp.where(lane == 2 * f + 1, pltpu.roll(cells, 2 * f + 2, 1), tail)

    row_out2[0] = jnp.concatenate([u[pl.ds(ROWS - 1, SLAB, stride=ROWS), :], blank], 0).astype(BF16)
    row_out2[1] = jnp.concatenate([u[pl.ds(0, SLAB, stride=ROWS), :], blank], 0).astype(BF16)
    col_out2[0] = tail.astype(BF16)
    col_out2[1] = head.astype(BF16)
    halo = exchange(
        (row_out2.at[0], row_out2.at[1], col_out2.at[0], col_out2.at[1]),
        (row_in2.at[0], row_in2.at[1], col_in2.at[0], col_in2.at[1]),
        halo_send2,
        halo_recv2,
    )
    ends = jnp.logical_or(lane == 0, lane == LANES - 1)
    for f in range(FIELDS):
        here = pl.ds(f * ROWS, ROWS)
        cells = field(u, f)
        new_ref[here, :] = cells
        upper = jnp.where(row == 0, jnp.where(first_x, cells, 0.0), pltpu.roll(cells, 1, 0))
        lower = jnp.where(
            row == ROWS - 1, jnp.where(last_x, cells, 0.0), pltpu.roll(cells, ROWS - 1, 0)
        )
        left = jnp.where(lane == 0, jnp.where(first_y, cells, 0.0), pltpu.roll(cells, 1, 1))
        right = jnp.where(
            lane == LANES - 1, jnp.where(last_y, cells, 0.0), pltpu.roll(cells, LANES - 1, 1)
        )
        flux_ref[here, :] = kappa[f] * (upper + lower + left + right - 4.0 * cells)
    exchanged(halo)
    norths = jnp.where(first_x, 0.0, row_in2[0].astype(F32))
    souths = jnp.where(last_x, 0.0, row_in2[1].astype(F32))
    sides = jnp.where(first_y, 0.0, col_in2[0].astype(F32)) + jnp.where(
        last_y, 0.0, col_in2[1].astype(F32)
    )
    for f in range(FIELDS):
        here = pl.ds(f * ROWS, ROWS)
        outer = jnp.where(ends, pltpu.roll(sides, LANES - 1 - 2 * f, 1), 0.0)
        outer = outer + jnp.where(row == 0, norths[f : f + 1, :], 0.0)
        outer = outer + jnp.where(row == ROWS - 1, souths[f : f + 1, :], 0.0)
        flux_ref[here, :] += kappa[f] * outer

    for n, (out, _, tiles) in enumerate(messages):
        whole = pl.ds(0, tiles * (count - 1))
        pltpu.make_async_copy(out.at[whole], out.at[whole], send_sem.at[n]).wait()


def finish(cells, flux, cells_out, flux_out, sem):
    copies = [
        pltpu.make_async_copy(cells, cells_out, sem.at[0]),
        pltpu.make_async_copy(flux, flux_out, sem.at[1]),
    ]
    for copy in copies:
        copy.start()
    for copy in copies:
        copy.wait()


def shards(nx, ny, old_fields, send_block, pair_slot, pair_block, crossing, kappa):
    shape = old_fields.shape
    count = nx * ny
    flat = (FIELDS * ROWS, LANES)
    padded = (SLAB * ROWS, LANES)
    hbm = pl.BlockSpec(memory_space=pltpu.HBM)
    vmem = pl.BlockSpec(memory_space=pltpu.VMEM)
    in_hbm = lambda array: pltpu.with_memory_space_constraint(array, pltpu.HBM)
    cells, fluxes = pl.pallas_call(
        functools.partial(kernel, nx, ny),
        out_shape=(
            jax.ShapeDtypeStruct(flat, F32),
            jax.ShapeDtypeStruct(flat, F32),
        ),
        in_specs=[hbm] * 6,
        out_specs=(vmem, vmem),
        scratch_shapes=[
            pltpu.VMEM(padded, F32),
            pltpu.VMEM(flat, F32),
            pltpu.VMEM((2, ROWS, LANES), F32),
            pltpu.VMEM((8 * ROWS, LANES), F32),
            pltpu.VMEM((ROWS, FULL, LANES), BF16),
            pltpu.VMEM((ROWS, FULL, LANES), BF16),
            pltpu.VMEM((ROWS, 8, LANES), F32),
            pltpu.VMEM((2, ROWS, LANES), F32),
            pltpu.VMEM((2 * count, 16, LANES), BF16),
            pltpu.VMEM((2 * count, 16, LANES), BF16),
            pltpu.VMEM((count, 8, LANES), BF16),
            pltpu.VMEM((count, 1, LANES), F32),
            pltpu.VMEM((2 * count, 16, LANES), BF16),
            pltpu.VMEM((2 * count, 16, LANES), BF16),
            pltpu.VMEM((count, 8, LANES), BF16),
            pltpu.VMEM((count, 1, LANES), F32),
            pltpu.VMEM((count, LANES), F32),
            pltpu.VMEM((CAP * count, SLAB, LANES), F32),
            pltpu.SMEM((1, CAP * count), jnp.int32),
            pltpu.SMEM((1, PAIRS), jnp.int32),
            pltpu.VMEM((1, PAIRS), jnp.int32),
            pltpu.SMEM((FIELDS,), F32),
            pltpu.VMEM((PAIRS, 3 * LANES, LANES), BF16),
            pltpu.VMEM((PAIRS * SLAB, LANES), F32),
            pltpu.VMEM((ROWS, LANES), F32),
            pltpu.VMEM((2, SLAB, LANES), F32),
            pltpu.VMEM((2, SLAB, LANES), F32),
            pltpu.VMEM((2, ROWS, LANES), F32),
            pltpu.VMEM((2, ROWS, LANES), F32),
            pltpu.VMEM((2, 32, LANES), BF16),
            pltpu.VMEM((2, 32, LANES), BF16),
            pltpu.VMEM((2, ROWS, LANES), BF16),
            pltpu.VMEM((2, ROWS, LANES), BF16),
            pltpu.SemaphoreType.DMA((6,)),
            pltpu.SemaphoreType.DMA((4,)),
            pltpu.SemaphoreType.DMA((4,)),
            pltpu.SemaphoreType.DMA((4,)),
            pltpu.SemaphoreType.DMA((4,)),
            pltpu.SemaphoreType.DMA((4,)),
            pltpu.SemaphoreType.DMA((4,)),
        ],
        compiler_params=pltpu.CompilerParams(
            collective_id=0, has_side_effects=True, vmem_limit_bytes=48 * 2**20
        ),
        cost_estimate=pl.CostEstimate(
            flops=2 * PAIRS * 3 * LANES * LANES * SLAB,
            bytes_accessed=12 * 2**20,
            transcendentals=0,
        ),
    )(
        in_hbm(old_fields.reshape(flat)),
        in_hbm(crossing.reshape(PAIRS, 3 * LANES, LANES)),
        in_hbm(send_block),
        in_hbm(pair_slot),
        in_hbm(pair_block),
        in_hbm(kappa),
    )
    new_fields, flux = pl.pallas_call(
        finish,
        out_shape=(jax.ShapeDtypeStruct(flat, F32), jax.ShapeDtypeStruct(flat, F32)),
        in_specs=[vmem, vmem],
        out_specs=(hbm, hbm),
        scratch_shapes=[pltpu.SemaphoreType.DMA((2,))],
        compiler_params=pltpu.CompilerParams(vmem_limit_bytes=4 * 2**20),
    )(cells, fluxes)
    return new_fields.reshape(shape), flux.reshape(shape)


def solution(mesh):
    placed = (
        P(None, "gx", "gy"),
        P(("gx", "gy"), None),
        P(("gx", "gy"), None),
        P(("gx", "gy"), None),
        P(("gx", "gy"), None, None, None, None),
        P(),
    )
    return jax.shard_map(
        functools.partial(shards, mesh.shape["gx"], mesh.shape["gy"]),
        mesh=mesh,
        in_specs=placed,
        out_specs=(P(None, "gx", "gy"), P(None, "gx", "gy")),
        check_vma=False,
    )
```

```python
import functools

import jax
import jax.numpy as jnp
from jax import lax
from jax.experimental import pallas as pl
from jax.experimental.pallas import tpu as pltpu
from jax.sharding import PartitionSpec as P

MESH = pl.DeviceIdType.MESH
F32 = jnp.float32
BF16 = jnp.bfloat16

FIELDS = 18
FULL = 16
ROWS = 64
LANES = 128
PAIRS = 112
CAP = 2
SLAB = 24
VOLUME = 18


def chip_offsets():
    groups, seen = [], {(0, 0, 0)}
    for code in range(1, 64):
        offset = (code // 16, code // 4 % 4, code % 4)
        group = []
        for sign in (1, -1):
            for turn in range(3):
                other = tuple(sign * offset[(turn + axis) % 3] % 4 for axis in range(3))
                if other not in seen:
                    seen.add(other)
                    group.append(other)
        if group:
            groups.append(group)
    groups.sort(key=lambda group: -sum(min(step, 4 - step) for step in group[0]))
    codes = [kx + 4 * ky + 16 * kz for group in groups for kx, ky, kz in group]
    return [sum(codes[n + m] * 64**m for m in range(3)) for n in range(0, len(codes), 3)]


ORDER = chip_offsets()


def minmod(first, second):
    least = jnp.where(first > 0.0, jnp.minimum(first, second), jnp.maximum(first, second))
    return jnp.where(first * second > 0.0, least, jnp.zeros_like(first))


def iota(shape, axis):
    return lax.broadcasted_iota(jnp.int32, shape, axis)


def loop(count, step, body):
    def outer(n, carry):
        for part in range(step):
            body(n * step + part)
        return carry

    lax.fori_loop(0, count // step, outer, 0)


def kernel(
    nx,
    ny,
    old_hbm,
    crossing_hbm,
    wanted_hbm,
    slots_hbm,
    blocks_hbm,
    kappa_hbm,
    new_ref,
    flux_ref,
    u,
    gx,
    inner,
    rest,
    table_u,
    table_g,
    table_lo,
    table_e,
    send_a,
    send_b,
    send_c,
    send_e,
    recv_a,
    recv_b,
    recv_c,
    recv_e,
    end_rows,
    pair_rows,
    wanted,
    slots,
    blocks,
    kappa,
    weights,
    contrib,
    volume,
    row_out,
    row_in,
    col_out,
    col_in,
    row_out2,
    row_in2,
    col_out2,
    col_in2,
    local_sem,
    halo_send,
    halo_recv,
    halo_send2,
    halo_recv2,
    send_sem,
    recv_sem,
):
    i = lax.axis_index("gx")
    j = lax.axis_index("gy")
    count = nx * ny
    me = i * ny + j

    get_old = pltpu.make_async_copy(old_hbm, u.at[pl.ds(0, FIELDS * ROWS)], local_sem.at[0])
    get_old.start()
    small = []
    for n, (source, target) in enumerate(
        ((wanted_hbm, wanted), (slots_hbm, slots), (blocks_hbm, blocks), (kappa_hbm, kappa))
    ):
        copy = pltpu.make_async_copy(source, target, local_sem.at[2 + n])
        copy.start()
        small.append(copy)
    get_weights = pltpu.make_async_copy(crossing_hbm, weights, local_sem.at[1])
    get_weights.start()

    barrier = pltpu.get_barrier_semaphore()

    def greet(k, carry):
        for core in range(2):
            di = lax.rem(i // 4 + 2 + k // 4, 4) * 4 + lax.rem(i + 2 + k, 4)
            dj = lax.rem(lax.rem(j, 2) + core, 2)
            for step in range(4):
                signal(di, lax.rem(j // 2 + 2 + step, 4) * 2 + dj)
        return carry

    def signal(di, dj):
        @pl.when(di * ny + dj != me)
        def _():
            pl.semaphore_signal(barrier, inc=1, device_id=(di, dj), device_id_type=MESH)

    lax.fori_loop(0, nx, greet, 0)

    after_x = (lax.rem(i + 1, nx), j)
    before_x = (lax.rem(i + nx - 1, nx), j)
    after_y = (i, lax.rem(j + 1, ny))
    before_y = (i, lax.rem(j + ny - 1, ny))
    first_x, last_x = i == 0, i == nx - 1
    first_y, last_y = j == 0, j == ny - 1

    lane = iota((ROWS, LANES), 1)
    row = iota((ROWS, LANES), 0)

    def field(ref, f):
        return ref[pl.ds(f * ROWS, ROWS), :]

    zeros = jnp.zeros((ROWS, LANES), F32)
    for f in range(FIELDS, SLAB):
        u[pl.ds(f * ROWS, ROWS), :] = zeros
    for f in range(4, 8):
        rest[pl.ds(f * ROWS, ROWS), :] = zeros
    get_old.wait()
    row_out[0] = u[pl.ds(ROWS - 1, SLAB, stride=ROWS), :]
    row_out[1] = u[pl.ds(0, SLAB, stride=ROWS), :]
    columns = [zeros] * 4
    for f in range(FIELDS):
        cells = field(u, f)
        for n, back in enumerate((0, 1, LANES - 2, LANES - 1)):
            shift = (f - back) % LANES
            moved = pltpu.roll(cells, shift, 1) if shift else cells
            columns[n] = jnp.where(lane == f, moved, columns[n])
    col_out[0] = columns[3]
    col_out[1] = columns[0]
    inner[0] = columns[1]
    inner[1] = columns[2]

    def value_row(r):
        table_u[r] = u[pl.ds(r, FULL, stride=ROWS), :].astype(BF16)

    loop(ROWS, 8, value_row)

    pl.semaphore_wait(barrier, count - 1)

    def exchange(sources, targets, sends, receives):
        copies = []
        for n, device in enumerate((after_x, before_x, after_y, before_y)):
            copy = pltpu.make_async_remote_copy(
                src_ref=sources[n],
                dst_ref=targets[n],
                send_sem=sends.at[n],
                recv_sem=receives.at[n],
                device_id=device,
                device_id_type=MESH,
            )
            copies.append(copy)
        return copies

    def start_exchange(copies, which):
        for n in which:
            pl.when(jnp.logical_not((last_x, first_x, last_y, first_y)[n]))(copies[n].start)

    def exchanged(copies):
        for n, copy in enumerate(copies):
            pl.when(jnp.logical_not((last_x, first_x, last_y, first_y)[n]))(copy.wait_send)
            pl.when(jnp.logical_not((first_x, last_x, first_y, last_y)[n]))(copy.wait_recv)

    halo = exchange(
        (row_out.at[0], row_out.at[1], col_out.at[0], col_out.at[1]),
        (row_in.at[0], row_in.at[1], col_in.at[0], col_in.at[1]),
        halo_send,
        halo_recv,
    )
    start_exchange(halo, range(4))

    y, z = i // 4, lax.rem(i, 4)
    x, c = j // 2, lax.rem(j, 2)

    def to_partners(body, together):
        def visit(kx, ky, kz, kc):
            di = lax.rem(y + ky, 4) * 4 + lax.rem(z + kz, 4)
            dj = lax.rem(x + kx, 4) * 2 + lax.rem(c + kc, 2)
            body(di * ny + dj, (di, dj))

        def some(n, carry):
            at = lax.rem(n, len(ORDER))
            word = jnp.int32(ORDER[0])
            for m in range(1, len(ORDER)):
                word = jnp.where(at == m, jnp.int32(ORDER[m]), word)
            for part in range(3):
                code = word // 64**part
                kx, ky, kz = lax.rem(code, 4), lax.rem(code // 4, 4), lax.rem(code // 16, 4)
                for kc in (0, 1) if together else (n // len(ORDER),):
                    visit(kx, ky, kz, kc)
            return carry

        lax.fori_loop(0, len(ORDER), some, 0)
        visit(0, 0, 0, 1)
        if not together:
            lax.fori_loop(len(ORDER), 2 * len(ORDER), some, 0)

    def row_of(d, slot):
        return jnp.maximum(wanted[0, d * CAP + slot], 0)

    def pack_a(ref, at, d):
        ref[2 * at] = table_u[row_of(d, 0)]
        ref[2 * at + 1] = table_u[row_of(d, 1)]

    def send(*parts, together=True):
        def one(d, device):
            for n, tiles, pack, out, landed in parts:
                pack(out, d, d)
                pltpu.make_async_remote_copy(
                    src_ref=out.at[pl.ds(tiles * d, tiles)],
                    dst_ref=landed.at[pl.ds(tiles * me, tiles)],
                    send_sem=send_sem.at[n],
                    recv_sem=recv_sem.at[n],
                    device_id=device,
                    device_id_type=MESH,
                ).start()

        to_partners(one, together)
        for n, tiles, pack, out, landed in parts:
            pack(landed, me, me)

    small[0].wait()
    send((0, 2, pack_a, send_a, recv_a), together=False)

    exchanged(halo)
    for f in range(FIELDS):
        cells = field(u, f)
        north = jnp.where(first_x, cells[0:1, :], row_in[0, f : f + 1, :])
        south = jnp.where(last_x, cells[ROWS - 1 :, :], row_in[1, f : f + 1, :])
        upper = jnp.where(row == 0, north, pltpu.roll(cells, 1, 0))
        lower = jnp.where(row == ROWS - 1, south, pltpu.roll(cells, ROWS - 1, 0))
        grad = minmod(lower - cells, cells - upper)
        gx[pl.ds(f * ROWS, ROWS), :] = grad
        if f >= FULL:
            rest[pl.ds((f - FULL) * ROWS, ROWS), :] = cells
            rest[pl.ds((2 + f - FULL) * ROWS, ROWS), :] = grad

    head, tail = col_out[1], col_out[0]
    west = jnp.where(first_y, head, col_in[0])
    east = jnp.where(last_y, tail, col_in[1])
    edges = minmod(inner[0] - head, head - west)
    edges = jnp.where(
        lane < SLAB, edges, pltpu.roll(minmod(east - tail, tail - inner[1]), SLAB, 1)
    )
    edges = jnp.where(lane < 2 * SLAB, edges, 0.0)
    table_e[0] = edges
    table_e[1] = pltpu.roll(edges, 64, 1)

    small_lane = iota((8, LANES), 1)
    small_row = iota((8, LANES), 0)

    def gradient_row(r):
        table_g[r] = gx[pl.ds(r, FULL, stride=ROWS), :].astype(BF16)
        table_lo[r] = rest[pl.ds(r, 8, stride=ROWS), :]

    loop(ROWS, 8, gradient_row)

    def pack_c(ref, at, d):
        low = jnp.where(
            small_row < 4, table_lo[row_of(d, 0)], pltpu.roll(table_lo[row_of(d, 1)], 4, 0)
        )
        ref[at] = low.astype(BF16)

    def pack_e(ref, at, d):
        ref[at] = table_e[0, pl.ds(row_of(d, 0), 1), :] + table_e[1, pl.ds(row_of(d, 1), 1), :]

    send((1, 1, pack_c, send_c, recv_c), (3, 1, pack_e, send_e, recv_e))

    def pack_b(ref, at, d):
        ref[2 * at] = table_g[row_of(d, 0)]
        ref[2 * at + 1] = table_g[row_of(d, 1)]

    send((2, 2, pack_b, send_b, recv_b))

    for copy in small[1:]:
        copy.wait()
    get_weights.wait()
    messages = (
        (send_a, recv_a, 2),
        (send_c, recv_c, 1),
        (send_b, recv_b, 2),
        (send_e, recv_e, 1),
    )

    def landed_whole(n):
        _, landed, tiles = messages[n]
        whole = pl.ds(0, tiles * (count - 1))
        pltpu.make_async_copy(landed.at[whole], landed.at[whole], recv_sem.at[n]).wait()

    def grad_y(cells):
        lanes = iota(cells.shape, 1)
        step = pltpu.roll(cells, LANES - 1, 1) - cells
        inside = jnp.logical_and(lanes > 0, lanes < LANES - 1)
        return jnp.where(inside, minmod(step, pltpu.roll(step, 1, 1)), 0.0)

    def slab(p, size, start=0):
        return pl.ds(pl.multiple_of(p * SLAB + start, 8), size)

    def weight(p, k):
        return weights[p, pl.ds(k * LANES, LANES), :]

    def upper_terms(p):
        values = recv_a[slots[0, p]]
        return jnp.concatenate([values, grad_y(values.astype(F32)).astype(BF16)], 1)

    def upper_product(q):
        p = 2 * q
        left = jnp.concatenate([upper_terms(p), upper_terms(p + 1)], 0)
        right = [jnp.concatenate([weight(n, 0), weight(n, 2)], 0) for n in (p, p + 1)]
        both = jnp.dot(left, jnp.concatenate(right, 1), preferred_element_type=F32)
        contrib[slab(p, FULL), :] = both[:FULL, :LANES]
        contrib[slab(p + 1, FULL), :] = both[FULL:, LANES:]

    def end_weights(p):
        end_rows[pl.ds(p, 1), :] = weights[p, pl.ds(2 * LANES, 16), :].astype(F32)[0:1]
        end_rows[pl.ds(LANES + p, 1), :] = weights[p, pl.ds(3 * LANES - 16, 16), :].astype(F32)[15:16]

    for ref, start in ((end_rows, 0), (end_rows, LANES), (pair_rows, 0)):
        ref[pl.ds(start + PAIRS, LANES - PAIRS), :] = jnp.zeros((LANES - PAIRS, LANES), F32)
    loop(PAIRS, 8, end_weights)
    landed_whole(0)
    loop(PAIRS // 2, 7, upper_product)

    is_volume = small_row == VOLUME - FULL
    ones = jnp.ones((8, LANES), F32)
    blank = jnp.zeros((8, LANES), F32)

    def lower_terms(p):
        e = slots[0, p]
        low = recv_c[e // 2].astype(F32)
        low = jnp.where(lax.rem(e, 2) == 1, pltpu.roll(low, 4, 0), low)
        low_u = jnp.where(is_volume, ones, low)
        low_g = jnp.where(is_volume, blank, pltpu.roll(low, 6, 0))
        low_y = jnp.where(is_volume, blank, grad_y(low))
        return jnp.concatenate([low_u, low_g, low_y], 1)

    def lower_product(q):
        p = 2 * q
        left = jnp.concatenate([lower_terms(p), lower_terms(p + 1)], 0).astype(BF16)
        right = jnp.concatenate([weights[p], weights[p + 1]], 1)
        both = jnp.dot(left, right, preferred_element_type=F32)
        contrib[slab(p, 8, FULL), :] = both[:8, :LANES]
        contrib[slab(p + 1, 8, FULL), :] = both[8:, LANES:]

    landed_whole(1)
    loop(PAIRS // 2, 7, lower_product)

    landed_whole(3)

    def pair_row(p):
        e = slots[0, p]
        edges = recv_e[e // 2]
        pair_rows[pl.ds(p, 1), :] = jnp.where(lax.rem(e, 2) == 1, pltpu.roll(edges, 64, 1), edges)

    loop(PAIRS, 8, pair_row)
    turned = pair_rows[...].T
    chosen = (iota((ROWS, PAIRS), 0) == blocks[...]).astype(F32)
    wide = jnp.concatenate([chosen, jnp.zeros((ROWS, LANES - PAIRS), F32)], 1)
    chosen = chosen.astype(BF16)
    for start in range(0, FIELDS, 6):
        left = [
            jnp.concatenate([wide * turned[f : f + 1], wide * turned[SLAB + f : SLAB + f + 1]], 1)
            for f in range(start, start + 6)
        ]
        u[pl.ds(start * ROWS, 6 * ROWS), :] = jnp.dot(
            jnp.concatenate(left, 0).astype(BF16),
            end_rows[...].astype(BF16),
            preferred_element_type=F32,
        )

    def gathered(f):
        terms = contrib[pl.ds(f, PAIRS, stride=SLAB), :]
        high = terms.astype(BF16)
        low = (terms - high.astype(F32)).astype(BF16)
        return jnp.dot(chosen, high, preferred_element_type=F32) + jnp.dot(
            chosen, low, preferred_element_type=F32
        )

    volume[...] = 1.0 / gathered(VOLUME)
    for f in range(FIELDS):
        u[pl.ds(f * ROWS, ROWS), :] += gathered(f)

    landed_whole(2)

    def second_product(q):
        p = 2 * q
        left = jnp.concatenate([recv_b[slots[0, p]], recv_b[slots[0, p + 1]]], 0)
        middle = pl.ds(LANES, LANES)
        right = jnp.concatenate([weights[p, middle, :], weights[p + 1, middle, :]], 1)
        both = jnp.dot(left, right, preferred_element_type=F32)
        contrib[slab(p, FULL), :] = both[:FULL, :LANES]
        contrib[slab(p + 1, FULL), :] = both[FULL:, LANES:]

    loop(PAIRS // 2, PAIRS // 2, second_product)

    head, tail = zeros, zeros
    for f in range(FIELDS):
        cells = field(u, f)
        if f < FULL:
            cells = cells + gathered(f)
        cells = cells * volume[...]
        u[pl.ds(f * ROWS, ROWS), :] = cells

    row_out2[0] = jnp.concatenate([u[pl.ds(ROWS - 1, SLAB, stride=ROWS), :], blank], 0).astype(BF16)
    row_out2[1] = jnp.concatenate([u[pl.ds(0, SLAB, stride=ROWS), :], blank], 0).astype(BF16)
    halo = exchange(
        (row_out2.at[0], row_out2.at[1], col_out2.at[0], col_out2.at[1]),
        (row_in2.at[0], row_in2.at[1], col_in2.at[0], col_in2.at[1]),
        halo_send2,
        halo_recv2,
    )
    start_exchange(halo, (0, 1))
    for f in range(FIELDS):
        cells = field(u, f)
        head = jnp.where(lane == 2 * f, pltpu.roll(cells, 2 * f, 1) if f else cells, head)
        tail = jnp.where(lane == 2 * f + 1, pltpu.roll(cells, 2 * f + 2, 1), tail)
    col_out2[0] = tail.astype(BF16)
    col_out2[1] = head.astype(BF16)
    start_exchange(halo, (2, 3))
    ends = jnp.logical_or(lane == 0, lane == LANES - 1)
    for f in range(FIELDS):
        here = pl.ds(f * ROWS, ROWS)
        cells = field(u, f)
        new_ref[here, :] = cells
        upper = jnp.where(row == 0, jnp.where(first_x, cells, 0.0), pltpu.roll(cells, 1, 0))
        lower = jnp.where(
            row == ROWS - 1, jnp.where(last_x, cells, 0.0), pltpu.roll(cells, ROWS - 1, 0)
        )
        left = jnp.where(lane == 0, jnp.where(first_y, cells, 0.0), pltpu.roll(cells, 1, 1))
        right = jnp.where(
            lane == LANES - 1, jnp.where(last_y, cells, 0.0), pltpu.roll(cells, LANES - 1, 1)
        )
        flux_ref[here, :] = kappa[f] * (upper + lower + left + right - 4.0 * cells)
    exchanged(halo)
    norths = jnp.where(first_x, 0.0, row_in2[0].astype(F32))
    souths = jnp.where(last_x, 0.0, row_in2[1].astype(F32))
    sides = jnp.where(first_y, 0.0, col_in2[0].astype(F32)) + jnp.where(
        last_y, 0.0, col_in2[1].astype(F32)
    )
    for f in range(FIELDS):
        here = pl.ds(f * ROWS, ROWS)
        outer = jnp.where(ends, pltpu.roll(sides, LANES - 1 - 2 * f, 1), 0.0)
        outer = outer + jnp.where(row == 0, norths[f : f + 1, :], 0.0)
        outer = outer + jnp.where(row == ROWS - 1, souths[f : f + 1, :], 0.0)
        flux_ref[here, :] += kappa[f] * outer

    for n, (out, _, tiles) in enumerate(messages):
        whole = pl.ds(0, tiles * (count - 1))
        pltpu.make_async_copy(out.at[whole], out.at[whole], send_sem.at[n]).wait()


def finish(cells, flux, cells_out, flux_out, sem):
    copies = [
        pltpu.make_async_copy(cells, cells_out, sem.at[0]),
        pltpu.make_async_copy(flux, flux_out, sem.at[1]),
    ]
    for copy in copies:
        copy.start()
    for copy in copies:
        copy.wait()


def shards(nx, ny, old_fields, send_block, pair_slot, pair_block, crossing, kappa):
    shape = old_fields.shape
    count = nx * ny
    flat = (FIELDS * ROWS, LANES)
    padded = (SLAB * ROWS, LANES)
    hbm = pl.BlockSpec(memory_space=pltpu.HBM)
    vmem = pl.BlockSpec(memory_space=pltpu.VMEM)
    in_hbm = lambda array: pltpu.with_memory_space_constraint(array, pltpu.HBM)
    cells, fluxes = pl.pallas_call(
        functools.partial(kernel, nx, ny),
        out_shape=(
            jax.ShapeDtypeStruct(flat, F32),
            jax.ShapeDtypeStruct(flat, F32),
        ),
        in_specs=[hbm] * 6,
        out_specs=(vmem, vmem),
        scratch_shapes=[
            pltpu.VMEM(padded, F32),
            pltpu.VMEM(flat, F32),
            pltpu.VMEM((2, ROWS, LANES), F32),
            pltpu.VMEM((8 * ROWS, LANES), F32),
            pltpu.VMEM((ROWS, FULL, LANES), BF16),
            pltpu.VMEM((ROWS, FULL, LANES), BF16),
            pltpu.VMEM((ROWS, 8, LANES), F32),
            pltpu.VMEM((2, ROWS, LANES), F32),
            pltpu.VMEM((2 * count, 16, LANES), BF16),
            pltpu.VMEM((2 * count, 16, LANES), BF16),
            pltpu.VMEM((count, 8, LANES), BF16),
            pltpu.VMEM((count, 1, LANES), F32),
            pltpu.VMEM((2 * count, 16, LANES), BF16),
            pltpu.VMEM((2 * count, 16, LANES), BF16),
            pltpu.VMEM((count, 8, LANES), BF16),
            pltpu.VMEM((count, 1, LANES), F32),
            pltpu.VMEM((2 * LANES, LANES), F32),
            pltpu.VMEM((LANES, LANES), F32),
            pltpu.SMEM((1, CAP * count), jnp.int32),
            pltpu.SMEM((1, PAIRS), jnp.int32),
            pltpu.VMEM((1, PAIRS), jnp.int32),
            pltpu.SMEM((FIELDS,), F32),
            pltpu.VMEM((PAIRS, 3 * LANES, LANES), BF16),
            pltpu.VMEM((PAIRS * SLAB, LANES), F32),
            pltpu.VMEM((ROWS, LANES), F32),
            pltpu.VMEM((2, SLAB, LANES), F32),
            pltpu.VMEM((2, SLAB, LANES), F32),
            pltpu.VMEM((2, ROWS, LANES), F32),
            pltpu.VMEM((2, ROWS, LANES), F32),
            pltpu.VMEM((2, 32, LANES), BF16),
            pltpu.VMEM((2, 32, LANES), BF16),
            pltpu.VMEM((2, ROWS, LANES), BF16),
            pltpu.VMEM((2, ROWS, LANES), BF16),
            pltpu.SemaphoreType.DMA((6,)),
            pltpu.SemaphoreType.DMA((4,)),
            pltpu.SemaphoreType.DMA((4,)),
            pltpu.SemaphoreType.DMA((4,)),
            pltpu.SemaphoreType.DMA((4,)),
            pltpu.SemaphoreType.DMA((4,)),
            pltpu.SemaphoreType.DMA((4,)),
        ],
        compiler_params=pltpu.CompilerParams(
            collective_id=0, has_side_effects=True, vmem_limit_bytes=48 * 2**20
        ),
        cost_estimate=pl.CostEstimate(
            flops=2 * PAIRS * 3 * LANES * LANES * SLAB,
            bytes_accessed=12 * 2**20,
            transcendentals=0,
        ),
    )(
        in_hbm(old_fields.reshape(flat)),
        in_hbm(crossing.reshape(PAIRS, 3 * LANES, LANES)),
        in_hbm(send_block),
        in_hbm(pair_slot),
        in_hbm(pair_block),
        in_hbm(kappa),
    )
    new_fields, flux = pl.pallas_call(
        finish,
        out_shape=(jax.ShapeDtypeStruct(flat, F32), jax.ShapeDtypeStruct(flat, F32)),
        in_specs=[vmem, vmem],
        out_specs=(hbm, hbm),
        scratch_shapes=[pltpu.SemaphoreType.DMA((2,))],
        compiler_params=pltpu.CompilerParams(vmem_limit_bytes=4 * 2**20),
    )(cells, fluxes)
    return new_fields.reshape(shape), flux.reshape(shape)


def solution(mesh):
    placed = (
        P(None, "gx", "gy"),
        P(("gx", "gy"), None),
        P(("gx", "gy"), None),
        P(("gx", "gy"), None),
        P(("gx", "gy"), None, None, None, None),
        P(),
    )
    return jax.shard_map(
        functools.partial(shards, mesh.shape["gx"], mesh.shape["gy"]),
        mesh=mesh,
        in_specs=placed,
        out_specs=(P(None, "gx", "gy"), P(None, "gx", "gy")),
        check_vma=False,
    )
```

```python
import functools

import jax
import jax.numpy as jnp
from jax import lax
from jax.experimental import pallas as pl
from jax.experimental.pallas import tpu as pltpu
from jax.sharding import PartitionSpec as P

MESH = pl.DeviceIdType.MESH
F32 = jnp.float32
BF16 = jnp.bfloat16

FIELDS = 18
FULL = 16
ROWS = 64
LANES = 128
PAIRS = 112
CAP = 2
SLAB = 24
VOLUME = 18
PIECES = 6


def chip_offsets():
    groups, seen = [], {(0, 0, 0)}
    for code in range(1, 64):
        offset = (code // 16, code // 4 % 4, code % 4)
        group = []
        for sign in (1, -1):
            for turn in range(3):
                other = tuple(sign * offset[(turn + axis) % 3] % 4 for axis in range(3))
                if other not in seen:
                    seen.add(other)
                    group.append(other)
        if group:
            groups.append(group)
    groups.sort(key=lambda group: -sum(min(step, 4 - step) for step in group[0]))
    codes = [kx + 4 * ky + 16 * kz for group in groups for kx, ky, kz in group]
    return [sum(codes[n + m] * 64**m for m in range(3)) for n in range(0, len(codes), 3)]


ORDER = chip_offsets()


def minmod(first, second):
    least = jnp.where(first > 0.0, jnp.minimum(first, second), jnp.maximum(first, second))
    return jnp.where(first * second > 0.0, least, jnp.zeros_like(first))


def iota(shape, axis):
    return lax.broadcasted_iota(jnp.int32, shape, axis)


def loop(count, step, body):
    def outer(n, carry):
        for part in range(step):
            body(n * step + part)
        return carry

    lax.fori_loop(0, count // step, outer, 0)


def kernel(
    nx,
    ny,
    old_hbm,
    crossing_hbm,
    wanted_hbm,
    slots_hbm,
    blocks_hbm,
    kappa_hbm,
    new_ref,
    flux_ref,
    u,
    gx,
    inner,
    rest,
    table_u,
    table_g,
    table_lo,
    table_e,
    send_a,
    send_b,
    send_c,
    send_e,
    recv_a,
    recv_b,
    recv_c,
    recv_e,
    end_rows,
    pair_rows,
    wanted,
    slots,
    blocks,
    kappa,
    weights,
    contrib,
    volume,
    row_out,
    row_in,
    col_out,
    col_in,
    row_out2,
    row_in2,
    col_out2,
    col_in2,
    local_sem,
    halo_send,
    halo_recv,
    halo_send2,
    halo_recv2,
    send_sem,
    recv_sem,
):
    i = lax.axis_index("gx")
    j = lax.axis_index("gy")
    count = nx * ny
    me = i * ny + j

    get_old = pltpu.make_async_copy(old_hbm, u.at[pl.ds(0, FIELDS * ROWS)], local_sem.at[0])
    get_old.start()
    small = []
    for n, (source, target) in enumerate(
        ((wanted_hbm, wanted), (slots_hbm, slots), (blocks_hbm, blocks), (kappa_hbm, kappa))
    ):
        copy = pltpu.make_async_copy(source, target, local_sem.at[2 + n])
        copy.start()
        small.append(copy)
    get_weights = pltpu.make_async_copy(crossing_hbm, weights, local_sem.at[1])
    get_weights.start()

    barrier = pltpu.get_barrier_semaphore()

    def greet(k, carry):
        for core in range(2):
            di = lax.rem(i // 4 + 2 + k // 4, 4) * 4 + lax.rem(i + 2 + k, 4)
            dj = lax.rem(lax.rem(j, 2) + core, 2)
            for step in range(4):
                signal(di, lax.rem(j // 2 + 2 + step, 4) * 2 + dj)
        return carry

    def signal(di, dj):
        @pl.when(di * ny + dj != me)
        def _():
            pl.semaphore_signal(barrier, inc=1, device_id=(di, dj), device_id_type=MESH)

    for k in range(nx):
        greet(k, 0)

    after_x = (lax.rem(i + 1, nx), j)
    before_x = (lax.rem(i + nx - 1, nx), j)
    after_y = (i, lax.rem(j + 1, ny))
    before_y = (i, lax.rem(j + ny - 1, ny))
    first_x, last_x = i == 0, i == nx - 1
    first_y, last_y = j == 0, j == ny - 1

    lane = iota((ROWS, LANES), 1)
    row = iota((ROWS, LANES), 0)

    def field(ref, f):
        return ref[pl.ds(f * ROWS, ROWS), :]

    zeros = jnp.zeros((ROWS, LANES), F32)
    for f in range(FIELDS, SLAB):
        u[pl.ds(f * ROWS, ROWS), :] = zeros
    for f in range(4, 8):
        rest[pl.ds(f * ROWS, ROWS), :] = zeros
    get_old.wait()
    row_out[0] = u[pl.ds(ROWS - 1, SLAB, stride=ROWS), :]
    row_out[1] = u[pl.ds(0, SLAB, stride=ROWS), :]

    def columns(*places):
        found = [zeros] * len(places)
        for f in range(FIELDS):
            cells = field(u, f)
            for n, place in enumerate(places):
                shift = (f - place) % LANES
                moved = pltpu.roll(cells, shift, 1) if shift else cells
                found[n] = jnp.where(lane == f, moved, found[n])
        return found

    head, tail = columns(0, LANES - 1)
    col_out[0] = tail.astype(BF16)
    col_out[1] = head.astype(BF16)
    inner[2], inner[3] = head, tail

    def value_row(r):
        table_u[r] = u[pl.ds(r, FULL, stride=ROWS), :].astype(BF16)

    loop(ROWS, 8, value_row)

    pl.semaphore_wait(barrier, count - 1)

    def exchange(sources, targets, sends, receives):
        copies = []
        for n, device in enumerate((after_x, before_x, after_y, before_y)):
            copy = pltpu.make_async_remote_copy(
                src_ref=sources[n],
                dst_ref=targets[n],
                send_sem=sends.at[n],
                recv_sem=receives.at[n],
                device_id=device,
                device_id_type=MESH,
            )
            copies.append(copy)
        return copies

    def start_exchange(copies, which):
        for n in which:
            pl.when(jnp.logical_not((last_x, first_x, last_y, first_y)[n]))(copies[n].start)

    def exchanged(copies):
        for n, copy in enumerate(copies):
            pl.when(jnp.logical_not((last_x, first_x, last_y, first_y)[n]))(copy.wait_send)
            pl.when(jnp.logical_not((first_x, last_x, first_y, last_y)[n]))(copy.wait_recv)

    halo = exchange(
        (row_out.at[0], row_out.at[1], col_out.at[0], col_out.at[1]),
        (row_in.at[0], row_in.at[1], col_in.at[0], col_in.at[1]),
        halo_send,
        halo_recv,
    )
    start_exchange(halo, range(4))

    y, z = i // 4, lax.rem(i, 4)
    x, c = j // 2, lax.rem(j, 2)

    def to_partners(body, together):
        def visit(kx, ky, kz, kc):
            di = lax.rem(y + ky, 4) * 4 + lax.rem(z + kz, 4)
            dj = lax.rem(x + kx, 4) * 2 + lax.rem(c + kc, 2)
            body(di * ny + dj, (di, dj))

        def some(n, carry):
            at = lax.rem(n, len(ORDER))
            word = jnp.int32(ORDER[0])
            for m in range(1, len(ORDER)):
                word = jnp.where(at == m, jnp.int32(ORDER[m]), word)
            for part in range(3):
                code = word // 64**part
                kx, ky, kz = lax.rem(code, 4), lax.rem(code // 4, 4), lax.rem(code // 16, 4)
                for kc in (0, 1) if together else (n // len(ORDER),):
                    visit(kx, ky, kz, kc)
            return carry

        lax.fori_loop(0, len(ORDER), some, 0)
        visit(0, 0, 0, 1)
        if not together:
            lax.fori_loop(len(ORDER), 2 * len(ORDER), some, 0)

    def row_of(d, slot):
        return jnp.maximum(wanted[0, d * CAP + slot], 0)

    def pack_a(ref, at, d):
        ref[2 * at] = table_u[row_of(d, 0)]
        ref[2 * at + 1] = table_u[row_of(d, 1)]

    def send(*parts, together=True):
        def one(d, device):
            for n, tiles, pack, out, landed in parts:
                pack(out, d, d)
                pltpu.make_async_remote_copy(
                    src_ref=out.at[pl.ds(tiles * d, tiles)],
                    dst_ref=landed.at[pl.ds(tiles * me, tiles)],
                    send_sem=send_sem.at[n],
                    recv_sem=recv_sem.at[n],
                    device_id=device,
                    device_id_type=MESH,
                ).start()

        to_partners(one, together)
        for n, tiles, pack, out, landed in parts:
            pack(landed, me, me)

    small[0].wait()
    send((0, 2, pack_a, send_a, recv_a), together=False)

    inner[0], inner[1] = columns(1, LANES - 2)

    exchanged(halo)
    for f in range(FIELDS):
        cells = field(u, f)
        north = jnp.where(first_x, cells[0:1, :], row_in[0, f : f + 1, :])
        south = jnp.where(last_x, cells[ROWS - 1 :, :], row_in[1, f : f + 1, :])
        upper = jnp.where(row == 0, north, pltpu.roll(cells, 1, 0))
        lower = jnp.where(row == ROWS - 1, south, pltpu.roll(cells, ROWS - 1, 0))
        grad = minmod(lower - cells, cells - upper)
        gx[pl.ds(f * ROWS, ROWS), :] = grad
        if f >= FULL:
            rest[pl.ds((f - FULL) * ROWS, ROWS), :] = cells
            rest[pl.ds((2 + f - FULL) * ROWS, ROWS), :] = grad

    head, tail = inner[2], inner[3]
    west = jnp.where(first_y, head, col_in[0].astype(F32))
    east = jnp.where(last_y, tail, col_in[1].astype(F32))
    edges = minmod(inner[0] - head, head - west)
    edges = jnp.where(
        lane < SLAB, edges, pltpu.roll(minmod(east - tail, tail - inner[1]), SLAB, 1)
    )
    edges = jnp.where(lane < 2 * SLAB, edges, 0.0)
    table_e[0] = edges
    table_e[1] = pltpu.roll(edges, 64, 1)

    small_lane = iota((8, LANES), 1)
    small_row = iota((8, LANES), 0)

    def gradient_row(r):
        table_g[r] = gx[pl.ds(r, FULL, stride=ROWS), :].astype(BF16)
        table_lo[r] = rest[pl.ds(r, 8, stride=ROWS), :]

    loop(ROWS, 8, gradient_row)

    def pack_c(ref, at, d):
        low = jnp.where(
            small_row < 4, table_lo[row_of(d, 0)], pltpu.roll(table_lo[row_of(d, 1)], 4, 0)
        )
        ref[at] = low.astype(BF16)

    def pack_e(ref, at, d):
        ref[at] = table_e[0, pl.ds(row_of(d, 0), 1), :] + table_e[1, pl.ds(row_of(d, 1), 1), :]

    send((1, 1, pack_c, send_c, recv_c), (3, 1, pack_e, send_e, recv_e))

    def pack_b(ref, at, d):
        ref[2 * at] = table_g[row_of(d, 0)]
        ref[2 * at + 1] = table_g[row_of(d, 1)]

    send((2, 2, pack_b, send_b, recv_b), together=False)

    for copy in small[1:]:
        copy.wait()
    get_weights.wait()
    messages = (
        (send_a, recv_a, 2),
        (send_c, recv_c, 1),
        (send_b, recv_b, 2),
        (send_e, recv_e, 1),
    )

    def landed_whole(n):
        _, landed, tiles = messages[n]
        whole = pl.ds(0, tiles * (count - 1))
        pltpu.make_async_copy(landed.at[whole], landed.at[whole], recv_sem.at[n]).wait()

    def grad_y(cells):
        lanes = iota(cells.shape, 1)
        step = pltpu.roll(cells, LANES - 1, 1) - cells
        inside = jnp.logical_and(lanes > 0, lanes < LANES - 1)
        return jnp.where(inside, minmod(step, pltpu.roll(step, 1, 1)), 0.0)

    def slab(p, size, start=0):
        return pl.ds(pl.multiple_of(p * SLAB + start, 8), size)

    def weight(p, k):
        return weights[p, pl.ds(k * LANES, LANES), :]

    def upper_terms(p):
        values = recv_a[slots[0, p]]
        return jnp.concatenate([values, grad_y(values.astype(F32)).astype(BF16)], 1)

    def upper_product(q):
        p = 2 * q
        left = jnp.concatenate([upper_terms(p), upper_terms(p + 1)], 0)
        right = [jnp.concatenate([weight(n, 0), weight(n, 2)], 0) for n in (p, p + 1)]
        both = jnp.dot(left, jnp.concatenate(right, 1), preferred_element_type=F32)
        contrib[slab(p, FULL), :] = both[:FULL, :LANES]
        contrib[slab(p + 1, FULL), :] = both[FULL:, LANES:]

    def end_weights(p):
        end_rows[pl.ds(p, 1), :] = weights[p, pl.ds(2 * LANES, 16), :].astype(F32)[0:1]
        end_rows[pl.ds(LANES + p, 1), :] = weights[p, pl.ds(3 * LANES - 16, 16), :].astype(F32)[15:16]

    for ref, start in ((end_rows, 0), (end_rows, LANES), (pair_rows, 0)):
        ref[pl.ds(start + PAIRS, LANES - PAIRS), :] = jnp.zeros((LANES - PAIRS, LANES), F32)
    loop(PAIRS, 8, end_weights)
    landed_whole(0)
    loop(PAIRS // 2, 7, upper_product)

    is_volume = small_row == VOLUME - FULL
    ones = jnp.ones((8, LANES), F32)
    blank = jnp.zeros((8, LANES), F32)

    def lower_terms(p):
        e = slots[0, p]
        low = recv_c[e // 2].astype(F32)
        low = jnp.where(lax.rem(e, 2) == 1, pltpu.roll(low, 4, 0), low)
        low_u = jnp.where(is_volume, ones, low)
        low_g = jnp.where(is_volume, blank, pltpu.roll(low, 6, 0))
        low_y = jnp.where(is_volume, blank, grad_y(low))
        return jnp.concatenate([low_u, low_g, low_y], 1)

    def lower_product(q):
        p = 2 * q
        left = jnp.concatenate([lower_terms(p), lower_terms(p + 1)], 0).astype(BF16)
        right = jnp.concatenate([weights[p], weights[p + 1]], 1)
        both = jnp.dot(left, right, preferred_element_type=F32)
        contrib[slab(p, 8, FULL), :] = both[:8, :LANES]
        contrib[slab(p + 1, 8, FULL), :] = both[8:, LANES:]

    landed_whole(1)
    loop(PAIRS // 2, 7, lower_product)

    landed_whole(3)

    def pair_row(p):
        e = slots[0, p]
        edges = recv_e[e // 2]
        pair_rows[pl.ds(p, 1), :] = jnp.where(lax.rem(e, 2) == 1, pltpu.roll(edges, 64, 1), edges)

    loop(PAIRS, 8, pair_row)
    turned = pair_rows[...].T
    chosen = (iota((ROWS, PAIRS), 0) == blocks[...]).astype(F32)
    wide = jnp.concatenate([chosen, jnp.zeros((ROWS, LANES - PAIRS), F32)], 1)
    chosen = chosen.astype(BF16)
    for start in range(0, FIELDS, 6):
        left = [
            jnp.concatenate([wide * turned[f : f + 1], wide * turned[SLAB + f : SLAB + f + 1]], 1)
            for f in range(start, start + 6)
        ]
        u[pl.ds(start * ROWS, 6 * ROWS), :] = jnp.dot(
            jnp.concatenate(left, 0).astype(BF16),
            end_rows[...].astype(BF16),
            preferred_element_type=F32,
        )

    def gathered(f):
        terms = contrib[pl.ds(f, PAIRS, stride=SLAB), :]
        high = terms.astype(BF16)
        low = (terms - high.astype(F32)).astype(BF16)
        return jnp.dot(chosen, high, preferred_element_type=F32) + jnp.dot(
            chosen, low, preferred_element_type=F32
        )

    volume[...] = 1.0 / gathered(VOLUME)
    for f in range(FIELDS):
        u[pl.ds(f * ROWS, ROWS), :] += gathered(f)

    landed_whole(2)

    def second_product(q):
        p = 2 * q
        left = jnp.concatenate([recv_b[slots[0, p]], recv_b[slots[0, p + 1]]], 0)
        middle = pl.ds(LANES, LANES)
        right = jnp.concatenate([weights[p, middle, :], weights[p + 1, middle, :]], 1)
        both = jnp.dot(left, right, preferred_element_type=F32)
        contrib[slab(p, FULL), :] = both[:FULL, :LANES]
        contrib[slab(p + 1, FULL), :] = both[FULL:, LANES:]

    loop(PAIRS // 2, PAIRS // 2, second_product)

    head, tail = zeros, zeros
    for f in range(FIELDS):
        cells = field(u, f)
        if f < FULL:
            cells = cells + gathered(f)
        cells = cells * volume[...]
        u[pl.ds(f * ROWS, ROWS), :] = cells

    row_out2[0] = jnp.concatenate([u[pl.ds(ROWS - 1, SLAB, stride=ROWS), :], blank], 0).astype(BF16)
    row_out2[1] = jnp.concatenate([u[pl.ds(0, SLAB, stride=ROWS), :], blank], 0).astype(BF16)
    halo = exchange(
        (row_out2.at[0], row_out2.at[1], col_out2.at[0], col_out2.at[1]),
        (row_in2.at[0], row_in2.at[1], col_in2.at[0], col_in2.at[1]),
        halo_send2,
        halo_recv2,
    )
    start_exchange(halo, (0, 1))
    for f in range(FIELDS):
        cells = field(u, f)
        head = jnp.where(lane == 2 * f, pltpu.roll(cells, 2 * f, 1) if f else cells, head)
        tail = jnp.where(lane == 2 * f + 1, pltpu.roll(cells, 2 * f + 2, 1), tail)
    col_out2[0] = tail.astype(BF16)
    col_out2[1] = head.astype(BF16)
    start_exchange(halo, (2, 3))
    ends = jnp.logical_or(lane == 0, lane == LANES - 1)
    for f in range(FIELDS):
        here = pl.ds(f * ROWS, ROWS)
        cells = field(u, f)
        new_ref[here, :] = cells
        upper = jnp.where(row == 0, jnp.where(first_x, cells, 0.0), pltpu.roll(cells, 1, 0))
        lower = jnp.where(
            row == ROWS - 1, jnp.where(last_x, cells, 0.0), pltpu.roll(cells, ROWS - 1, 0)
        )
        left = jnp.where(lane == 0, jnp.where(first_y, cells, 0.0), pltpu.roll(cells, 1, 1))
        right = jnp.where(
            lane == LANES - 1, jnp.where(last_y, cells, 0.0), pltpu.roll(cells, LANES - 1, 1)
        )
        flux_ref[here, :] = kappa[f] * (upper + lower + left + right - 4.0 * cells)
    exchanged(halo)
    norths = jnp.where(first_x, 0.0, row_in2[0].astype(F32))
    souths = jnp.where(last_x, 0.0, row_in2[1].astype(F32))
    sides = jnp.where(first_y, 0.0, col_in2[0].astype(F32)) + jnp.where(
        last_y, 0.0, col_in2[1].astype(F32)
    )
    for f in range(FIELDS):
        here = pl.ds(f * ROWS, ROWS)
        outer = jnp.where(ends, pltpu.roll(sides, LANES - 1 - 2 * f, 1), 0.0)
        outer = outer + jnp.where(row == 0, norths[f : f + 1, :], 0.0)
        outer = outer + jnp.where(row == ROWS - 1, souths[f : f + 1, :], 0.0)
        flux_ref[here, :] += kappa[f] * outer

    for n, (out, _, tiles) in enumerate(messages):
        whole = pl.ds(0, tiles * (count - 1))
        pltpu.make_async_copy(out.at[whole], out.at[whole], send_sem.at[n]).wait()


def finish(cells, flux, cells_out, flux_out, sem):
    copies = []
    for source, target in ((cells, cells_out), (flux, flux_out)):
        for n in range(PIECES):
            part = pl.ds(n * FIELDS * ROWS // PIECES, FIELDS * ROWS // PIECES)
            copies.append(
                pltpu.make_async_copy(source.at[part], target.at[part], sem.at[len(copies)])
            )
    for copy in copies:
        copy.start()
    for copy in copies:
        copy.wait()


def shards(nx, ny, old_fields, send_block, pair_slot, pair_block, crossing, kappa):
    shape = old_fields.shape
    count = nx * ny
    flat = (FIELDS * ROWS, LANES)
    padded = (SLAB * ROWS, LANES)
    hbm = pl.BlockSpec(memory_space=pltpu.HBM)
    vmem = pl.BlockSpec(memory_space=pltpu.VMEM)
    in_hbm = lambda array: pltpu.with_memory_space_constraint(array, pltpu.HBM)
    cells, fluxes = pl.pallas_call(
        functools.partial(kernel, nx, ny),
        out_shape=(
            jax.ShapeDtypeStruct(flat, F32),
            jax.ShapeDtypeStruct(flat, F32),
        ),
        in_specs=[hbm] * 6,
        out_specs=(vmem, vmem),
        scratch_shapes=[
            pltpu.VMEM(padded, F32),
            pltpu.VMEM(flat, F32),
            pltpu.VMEM((4, ROWS, LANES), F32),
            pltpu.VMEM((8 * ROWS, LANES), F32),
            pltpu.VMEM((ROWS, FULL, LANES), BF16),
            pltpu.VMEM((ROWS, FULL, LANES), BF16),
            pltpu.VMEM((ROWS, 8, LANES), F32),
            pltpu.VMEM((2, ROWS, LANES), F32),
            pltpu.VMEM((2 * count, 16, LANES), BF16),
            pltpu.VMEM((2 * count, 16, LANES), BF16),
            pltpu.VMEM((count, 8, LANES), BF16),
            pltpu.VMEM((count, 1, LANES), F32),
            pltpu.VMEM((2 * count, 16, LANES), BF16),
            pltpu.VMEM((2 * count, 16, LANES), BF16),
            pltpu.VMEM((count, 8, LANES), BF16),
            pltpu.VMEM((count, 1, LANES), F32),
            pltpu.VMEM((2 * LANES, LANES), F32),
            pltpu.VMEM((LANES, LANES), F32),
            pltpu.SMEM((1, CAP * count), jnp.int32),
            pltpu.SMEM((1, PAIRS), jnp.int32),
            pltpu.VMEM((1, PAIRS), jnp.int32),
            pltpu.SMEM((FIELDS,), F32),
            pltpu.VMEM((PAIRS, 3 * LANES, LANES), BF16),
            pltpu.VMEM((PAIRS * SLAB, LANES), F32),
            pltpu.VMEM((ROWS, LANES), F32),
            pltpu.VMEM((2, SLAB, LANES), F32),
            pltpu.VMEM((2, SLAB, LANES), F32),
            pltpu.VMEM((2, ROWS, LANES), BF16),
            pltpu.VMEM((2, ROWS, LANES), BF16),
            pltpu.VMEM((2, 32, LANES), BF16),
            pltpu.VMEM((2, 32, LANES), BF16),
            pltpu.VMEM((2, ROWS, LANES), BF16),
            pltpu.VMEM((2, ROWS, LANES), BF16),
            pltpu.SemaphoreType.DMA((6,)),
            pltpu.SemaphoreType.DMA((4,)),
            pltpu.SemaphoreType.DMA((4,)),
            pltpu.SemaphoreType.DMA((4,)),
            pltpu.SemaphoreType.DMA((4,)),
            pltpu.SemaphoreType.DMA((4,)),
            pltpu.SemaphoreType.DMA((4,)),
        ],
        compiler_params=pltpu.CompilerParams(
            collective_id=0, has_side_effects=True, vmem_limit_bytes=48 * 2**20
        ),
        cost_estimate=pl.CostEstimate(
            flops=2 * PAIRS * 3 * LANES * LANES * SLAB,
            bytes_accessed=12 * 2**20,
            transcendentals=0,
        ),
    )(
        in_hbm(old_fields.reshape(flat)),
        in_hbm(crossing.reshape(PAIRS, 3 * LANES, LANES)),
        in_hbm(send_block),
        in_hbm(pair_slot),
        in_hbm(pair_block),
        in_hbm(kappa),
    )
    new_fields, flux = pl.pallas_call(
        finish,
        out_shape=(jax.ShapeDtypeStruct(flat, F32), jax.ShapeDtypeStruct(flat, F32)),
        in_specs=[vmem, vmem],
        out_specs=(hbm, hbm),
        scratch_shapes=[pltpu.SemaphoreType.DMA((2 * PIECES,))],
        compiler_params=pltpu.CompilerParams(vmem_limit_bytes=4 * 2**20),
    )(cells, fluxes)
    return new_fields.reshape(shape), flux.reshape(shape)


def solution(mesh):
    placed = (
        P(None, "gx", "gy"),
        P(("gx", "gy"), None),
        P(("gx", "gy"), None),
        P(("gx", "gy"), None),
        P(("gx", "gy"), None, None, None, None),
        P(),
    )
    return jax.shard_map(
        functools.partial(shards, mesh.shape["gx"], mesh.shape["gy"]),
        mesh=mesh,
        in_specs=placed,
        out_specs=(P(None, "gx", "gy"), P(None, "gx", "gy")),
        check_vma=False,
    )
```
